256 devices in a mesh: ta: 8 (over y, z_lo), gx: 4 (over x), gy: 8 (over z_hi, core).
Axes of the slice: x: 4, y: 4, z: 8 (z_hi: 4, z_lo: 2; z = z_hi * 2 + z_lo), core: 2. Of those that a mesh axis runs over, the one named last changes fastest.
Arguments:
- start_states: float32 [8, 256, 4096], P('ta', 'gx', 'gy'), may hold values from -6 to 6
- conduct: float32 [256, 4096], P('gx', 'gy'), may hold values from 0.5 to 2
- velocity: float32 [2, 256, 4096], P(None, 'gx', 'gy'), may hold values from -1 to 1
Outputs:
- end_states: float32 [8, 256, 4096], P('ta', 'gx', 'gy')
The draws below stay inside these ranges and needn't reach their ends.
All inputs are finite; a program needn't handle non-finite values.
Results may differ from the reference program's by a relative error of at most 0.00002.
Values sent between devices are 32-bit elements; how exact they have to be, the bound alone decides.
A program may use at most 64 MiB of HBM per device.

```python
import math
import jax
import jax.numpy as jnp

FINE = 2
NT = 8
NX = 256
NY = 4096


def shard_levels(rng, shape, cuts, least, top_value):
    gain, own = 1.0, jax.random.fold_in(rng, 6)
    for axis_at, parts in cuts:
        steps = jnp.exp(jax.random.uniform(jax.random.fold_in(own, axis_at), (parts,), jnp.float32, least / len(cuts), top_value / len(cuts)))
        gain = gain * jnp.repeat(steps, shape[axis_at] // parts).reshape([-1 if axis == axis_at else 1 for axis in range(len(shape))])
    return gain


def centred(rng, dims, spread, reach, shards=(), dtype=jnp.bfloat16):
    array = spread * jax.random.normal(rng, dims, jnp.float32)
    if shards:
        array = array * shard_levels(rng, dims, shards, -0.22, 0.18)
    return jnp.clip(array, -reach, reach).astype(dtype)


def setup_inputs(seed: int = 0) -> dict:
    key_of = jax.random.split(jax.random.key(seed), 4)
    start_states = centred(key_of[0], (NT, NX, NY), 1.0, 6.0, ((0, 8), (1, 4), (2, 8)), jnp.float32)
    conduct = jnp.clip(jnp.exp(math.log(2.0) - 1.3862944 * jax.random.uniform(key_of[1], (NX, NY), jnp.float32) ** shard_levels(key_of[1], (NX, NY), ((0, 4), (1, 8)), -0.2, 0.2)), 0.5, 2.0)
    velocity = jnp.clip(jax.random.uniform(key_of[2], (2, NX, NY), jnp.float32, -1.0, 1.0) * shard_levels(key_of[2], (2, NX, NY), ((1, 4), (2, 8)), -0.4, 0.0), -1.0, 1.0)
    return dict(start_states=start_states, conduct=conduct, velocity=velocity)


def element_rates(padded, kel, vxel, vyel):
    corner_a = padded[:-1, :-1]
    corner_b = padded[1:, :-1]
    corner_c = padded[:-1, 1:]
    corner_d = padded[1:, 1:]
    advect = 0.25 * (vxel * (0.5 * (corner_b + corner_d - corner_a - corner_c)) + vyel * (0.5 * (corner_c + corner_d - corner_a - corner_b)))
    stiff = kel / 6.0
    rate_a = stiff * (4.0 * corner_a - corner_b - corner_c - 2.0 * corner_d) + advect
    rate_b = stiff * (4.0 * corner_b - corner_a - corner_d - 2.0 * corner_c) + advect
    rate_c = stiff * (4.0 * corner_c - corner_a - corner_d - 2.0 * corner_b) + advect
    rate_d = stiff * (4.0 * corner_d - corner_b - corner_c - 2.0 * corner_a) + advect
    return rate_a[1:, 1:] + rate_b[:-1, 1:] + rate_c[1:, :-1] + rate_d[:-1, :-1]


def element_means(padded):
    return 0.25 * (padded[:, :-1, :-1] + padded[:, 1:, :-1] + padded[:, :-1, 1:] + padded[:, 1:, 1:])


def heun_step(field, step, elems):
    first = element_rates(jnp.pad(field, 1), elems[0], elems[1], elems[2])
    middle = field - step * first
    second = element_rates(jnp.pad(middle, 1), elems[0], elems[1], elems[2])
    return field - (0.5 * step) * (first + second)


def reference(start_states, conduct, velocity):
    coeffs = jnp.concatenate([conduct[None], velocity], axis=0)
    elems = element_means(jnp.pad(coeffs, ((0, 0), (1, 1), (1, 1))))
    deltas = []
    for section in range(NT):
        fine_state = start_states[section]
        for inner in range(FINE):
            fine_state = heun_step(fine_state, 0.1, elems)
        coarse_state = heun_step(start_states[section], 0.2, elems)
        deltas.append(fine_state - coarse_state)
    current = start_states[0]
    results = []
    for section in range(NT):
        current = heun_step(current, 0.2, elems) + deltas[section]
        results.append(current)
    return jnp.stack(results, axis=0)
```

```python
import functools

import jax
import jax.numpy as jnp
from jax import lax
from jax.experimental import pallas as pl
from jax.experimental.pallas import tpu as pltpu
from jax.sharding import PartitionSpec as P

MESH = pl.DeviceIdType.MESH
NT = 8
TR = 64
TC = 512
LT = 128
HB = 24
WR = TR + 2 * HB
DIRS = [(-1, -1), (-1, 0), (-1, 1), (0, -1), (0, 1), (1, -1), (1, 0), (1, 1)]
ROWS = [(0, 0, 0, 112), (1, 4, 8, 96), (5, 7, 16, 80)]


def row_span(section):
    for first, last, start, rows in ROWS:
        if first <= section <= last:
            return start, rows


def roll(value, shift, axis):
    return pltpu.roll(value, shift % value.shape[axis], axis)


def kernel(
    gxn, gyn, u_ref, cond_ref, vel_ref, out_ref,
    ubuf, wbuf, xbuf, main, other, cwin, cedge, coef, fsend, frecv,
    load_sem, su, ru, sc, rc, sx, rx, sf, rf,
):
    ta = lax.axis_index("ta")
    gx = lax.axis_index("gx")
    gy = lax.axis_index("gy")
    even = lax.rem(ta, 2) == 0
    tile_m = ta // 2
    tile_o = lax.rem(tile_m + jnp.where(even, 3, 1), 4)

    def has(dx, dy):
        x, y = gx + dx, gy + dy
        return (x >= 0) & (x < gxn) & (y >= 0) & (y < gyn)

    lanes_m = pl.ds(pl.multiple_of(tile_m * LT, LT), LT)
    lanes_o = pl.ds(pl.multiple_of(tile_o * LT, LT), LT)
    loads = [
        pltpu.make_async_copy(u_ref.at[0], ubuf.at[pl.ds(HB, TR), pl.ds(0, TC)], load_sem.at[0]),
        pltpu.make_async_copy(cond_ref.at[:, lanes_m], main.at[0], load_sem.at[1]),
        pltpu.make_async_copy(cond_ref.at[:, lanes_o], other.at[0], load_sem.at[2]),
        pltpu.make_async_copy(vel_ref.at[:, :, lanes_m], main.at[pl.ds(1, 2)], load_sem.at[3]),
        pltpu.make_async_copy(vel_ref.at[:, :, lanes_o], other.at[pl.ds(1, 2)], load_sem.at[4]),
    ]
    for load in loads:
        load.start()

    ubuf[0:HB, :] = jnp.zeros((HB, 6 * LT), jnp.float32)
    ubuf[HB + TR : WR, :] = jnp.zeros((HB, 6 * LT), jnp.float32)
    ubuf[HB : HB + TR, TC:] = jnp.zeros((TR, 2 * LT), jnp.float32)
    cwin[:, 0:HB, :] = jnp.zeros((3, HB, LT), jnp.float32)
    cwin[:, HB + TR : WR, :] = jnp.zeros((3, HB, LT), jnp.float32)
    cedge[...] = jnp.zeros((3, WR, LT), jnp.float32)

    barrier = pltpu.get_barrier_semaphore()
    count = NT - 1
    for dx, dy in DIRS:
        near = has(dx, dy)
        count = count + near.astype(jnp.int32)

        @pl.when(near)
        def _():
            pl.semaphore_signal(barrier, inc=1, device_id=(ta, gx + dx, gy + dy), device_id_type=MESH)

    for step in range(1, NT):
        pl.semaphore_signal(
            barrier, inc=1, device_id=(lax.rem(ta + step, NT), gx, gy), device_id_type=MESH
        )
    for load in loads:
        load.wait()

    lane = lax.broadcasted_iota(jnp.int32, (TR, LT), 1)
    use_m = jnp.where(even, lane, LT - 1 - lane) < 96
    for part in range(3):
        cwin[part, HB : HB + TR, :] = jnp.where(use_m, main[part], other[part])
    pl.semaphore_wait(barrier, count)

    src_rows = {-1: pl.ds(0, HB), 0: pl.ds(0, TR), 1: pl.ds(TR - HB, HB)}
    dst_rows = {-1: pl.ds(HB + TR, HB), 0: pl.ds(HB, TR), 1: pl.ds(0, HB)}
    src_cols = {-1: pl.ds(0, LT), 0: pl.ds(0, TC), 1: pl.ds(TC - LT, LT)}
    dst_cols = {-1: pl.ds(TC, LT), 0: pl.ds(0, TC), 1: pl.ds(TC + LT, LT)}
    own_rows = {-1: pl.ds(HB, HB), 0: pl.ds(HB, TR), 1: pl.ds(TR, HB)}

    def state_copy(at):
        dx, dy = DIRS[at]
        return pltpu.make_async_remote_copy(
            src_ref=ubuf.at[own_rows[dx], src_cols[dy]],
            dst_ref=ubuf.at[dst_rows[dx], dst_cols[dy]],
            send_sem=su.at[at],
            recv_sem=ru.at[at],
            device_id=(ta, gx + dx, gy + dy),
            device_id_type=MESH,
        )

    def coef_copy(at):
        dx, dy = DIRS[at]
        if dy == 0:
            src, dst = cwin.at[:, own_rows[dx], :], cwin.at[:, dst_rows[dx], :]
        else:
            src, dst = other.at[:, src_rows[dx], :], cedge.at[:, dst_rows[dx], :]
        return pltpu.make_async_remote_copy(
            src_ref=src,
            dst_ref=dst,
            send_sem=sc.at[at],
            recv_sem=rc.at[at],
            device_id=(ta, gx + dx, gy + dy),
            device_id_type=MESH,
        )

    def coef_goes(dy):
        return {-1: ta == NT - 1, 0: ta >= 0, 1: ta == 0}[dy]

    for at, (dx, dy) in enumerate(DIRS):

        @pl.when(has(dx, dy))
        def _():
            state_copy(at).start()

    for at, (dx, dy) in enumerate(DIRS):

        @pl.when(has(dx, dy) & coef_goes(dy))
        def _():
            coef_copy(at).start()

    for at, (dx, dy) in enumerate(DIRS):

        @pl.when(has(-dx, -dy))
        def _():
            state_copy(at).wait_recv()

    wlane = lax.broadcasted_iota(jnp.int32, (WR, LT), 1)
    for owner in range(NT):
        tile = owner // 2
        if owner % 2 == 0:
            mate = tile - 1 if tile else 5
            keep = wlane < 96
        else:
            mate = tile + 1
            keep = wlane >= 32
        window = jnp.where(
            keep, ubuf[:, tile * LT : (tile + 1) * LT], ubuf[:, mate * LT : (mate + 1) * LT]
        )
        wbuf[owner] = window

    def window_copy(owner, span):
        start, rows = span
        return pltpu.make_async_remote_copy(
            src_ref=wbuf.at[owner, pl.ds(start, rows)],
            dst_ref=xbuf.at[ta, pl.ds(start, rows)],
            send_sem=sx.at[owner],
            recv_sem=rx.at[ta],
            device_id=(owner, gx, gy),
            device_id_type=MESH,
        )

    for first, last, start, rows in ROWS:

        @pl.when((ta >= first) & (ta <= last))
        def _():
            for step in range(1, NT):
                window_copy(lax.rem(ta + step, NT), (start, rows)).start()

    xbuf[ta] = wbuf[ta]

    for at, (dx, dy) in enumerate(DIRS):

        @pl.when(has(-dx, -dy) & coef_goes(dy))
        def _():
            coef_copy(at).wait_recv()

    row = lax.broadcasted_iota(jnp.int32, (WR, LT), 0)
    keep_m = jnp.where(even, wlane, LT - 1 - wlane) < 96
    take_edge = jnp.logical_not(keep_m) & ((ta == 0) | (ta == NT - 1))

    def mean(part):
        value = jnp.where(take_edge, cedge[part], cwin[part])
        value = value + roll(value, -1, 1)
        return value + roll(value, -1, 0)

    stiff = mean(0) * (0.25 * 0.1 / 6.0)
    vx = mean(1) * (0.25 * 0.1 / 8.0)
    vy = mean(2) * (0.25 * 0.1 / 8.0)
    gam = vx + vy
    kap = vx - vy
    column = (
        gy * TC + ta * 64 + jnp.where(
            even,
            jnp.where(wlane < 96, wlane, wlane - LT),
            jnp.where(wlane < 32, wlane + 64, wlane - 64),
        )
    )
    line = gx * TR + row - HB
    inside = (column >= 0) & (column < gyn * TC) & (line >= 0) & (line < gxn * TR)

    def put(slot, shift, value):
        coef[slot] = roll(jnp.where(inside, value, 0.0), shift, 0)

    def before(value):
        return roll(value, 1, 0)

    def left(value):
        return roll(value, 1, 1)

    put(0, 0, (4.0 * stiff - gam) + before(4.0 * stiff + kap) + left(4.0 * stiff - kap + before(4.0 * stiff + gam)))
    put(1, 0, (-stiff - kap) + before(gam - stiff))
    put(2, 0, left((-stiff - gam) + before(kap - stiff)))
    put(3, 1, (kap - stiff) + left(gam - stiff))
    put(4, 1, gam - 2.0 * stiff)
    put(5, 1, left(kap - 2.0 * stiff))
    put(6, -1, before((-stiff - gam) + left(-stiff - kap)))
    put(7, -1, before(-kap - 2.0 * stiff))
    put(8, -1, left(before(-gam - 2.0 * stiff)))

    def rate(value, span):
        start, rows = span
        high = roll(value, -1, 1)
        low = roll(value, 1, 1)

        def line_sum(slot):
            return (
                coef[slot, start : start + rows] * value
                + coef[slot + 1, start : start + rows] * high
                + coef[slot + 2, start : start + rows] * low
            )

        return line_sum(0) + roll(line_sum(3), -1, 0) + roll(line_sum(6), 1, 0)

    def trim(value, old, new):
        skip = new[0] - old[0]
        return value[skip : skip + new[1]]

    def result_copy(section):
        return pltpu.make_async_remote_copy(
            src_ref=fsend.at[section],
            dst_ref=frecv.at[ta],
            send_sem=sf.at[section],
            recv_sem=rf.at[ta],
            device_id=(section, gx, gy),
            device_id_type=MESH,
        )

    flane = lax.broadcasted_iota(jnp.int32, (TR // 2, LT), 1)
    fmain = jnp.where(even, flane, LT - 1 - flane) < 64
    state, state_span = None, None
    for section in range(NT):
        span = row_span(section)
        start, rows = span

        @pl.when(ta != section)
        def _():
            pltpu.make_async_remote_copy(
                src_ref=wbuf.at[section, pl.ds(start, rows)],
                dst_ref=xbuf.at[section, pl.ds(start, rows)],
                send_sem=sx.at[section],
                recv_sem=rx.at[section],
                device_id=(section, gx, gy),
                device_id_type=MESH,
            ).wait_recv()

        value = xbuf[section, start : start + rows]
        r1 = rate(value, span)
        r2 = rate(r1, span)
        r3 = rate(r2, span)
        r4 = rate(r3, span)
        delta = 0.25 * r4 - r3
        if section == 0:
            state, state_span = value - 2.0 * (r1 - r2) + delta, span
        else:
            now = row_span(section + 1 if section == 4 else section)
            state = trim(state, state_span, now)
            first = rate(state, now)
            second = rate(first, now)
            state = state - 2.0 * (first - second) + trim(delta, span, now)
            state_span = now
        tile = trim(state, state_span, (HB, TR))
        folded = jnp.where(fmain, tile[: TR // 2], roll(tile[TR // 2 :], 64, 1))
        fsend[section] = folded

        @pl.when(ta != section)
        def _():
            result_copy(section).start()

    frecv[ta] = fsend[ta]

    for step in range(1, NT):
        peer = lax.rem(ta + step, NT)
        pltpu.make_async_remote_copy(
            src_ref=fsend.at[peer],
            dst_ref=frecv.at[peer],
            send_sem=sf.at[peer],
            recv_sem=rf.at[peer],
            device_id=(peer, gx, gy),
            device_id_type=MESH,
        ).wait_recv()

    for tile in range(4):
        lower, upper = frecv[2 * tile], frecv[2 * tile + 1]
        lanes = slice(tile * LT, (tile + 1) * LT)
        out_ref[0, : TR // 2, lanes] = jnp.where(flane < 64, lower, upper)
        out_ref[0, TR // 2 :, lanes] = roll(jnp.where(flane < 64, upper, lower), 64, 1)

    for at, (dx, dy) in enumerate(DIRS):

        @pl.when(has(dx, dy))
        def _():
            state_copy(at).wait_send()

        @pl.when(has(dx, dy) & coef_goes(dy))
        def _():
            coef_copy(at).wait_send()

    for first, last, start, rows in ROWS:

        @pl.when((ta >= first) & (ta <= last))
        def _():
            for step in range(1, NT):
                window_copy(lax.rem(ta + step, NT), (start, rows)).wait_send()

    for step in range(1, NT):
        result_copy(lax.rem(ta + step, NT)).wait_send()


def solution(mesh):
    gxn, gyn = mesh.shape["gx"], mesh.shape["gy"]

    def local(start_states, conduct, velocity):
        return pl.pallas_call(
            functools.partial(kernel, gxn, gyn),
            out_shape=jax.ShapeDtypeStruct((1, TR, TC), jnp.float32),
            in_specs=[pl.BlockSpec(memory_space=pl.ANY)] * 3,
            out_specs=pl.BlockSpec(memory_space=pltpu.VMEM),
            scratch_shapes=[
                pltpu.VMEM((WR, 6 * LT), jnp.float32),
                pltpu.VMEM((NT, WR, LT), jnp.float32),
                pltpu.VMEM((NT, WR, LT), jnp.float32),
                pltpu.VMEM((3, TR, LT), jnp.float32),
                pltpu.VMEM((3, TR, LT), jnp.float32),
                pltpu.VMEM((3, WR, LT), jnp.float32),
                pltpu.VMEM((3, WR, LT), jnp.float32),
                pltpu.VMEM((9, WR, LT), jnp.float32),
                pltpu.VMEM((NT, TR // 2, LT), jnp.float32),
                pltpu.VMEM((NT, TR // 2, LT), jnp.float32),
                pltpu.SemaphoreType.DMA((5,)),
            ]
            + [pltpu.SemaphoreType.DMA((8,))] * 8,
            compiler_params=pltpu.CompilerParams(
                collective_id=0, has_side_effects=True, vmem_limit_bytes=32 * 1024 * 1024
            ),
        )(start_states, conduct, velocity)

    in_specs = (P("ta", "gx", "gy"), P("gx", "gy"), P(None, "gx", "gy"))
    return jax.shard_map(
        local, mesh=mesh, in_specs=in_specs, out_specs=P("ta", "gx", "gy"), check_vma=False
    )
```

```python
import functools

import jax
import jax.numpy as jnp
from jax import lax
from jax.experimental import pallas as pl
from jax.experimental.pallas import tpu as pltpu
from jax.sharding import PartitionSpec as P

MESH = pl.DeviceIdType.MESH
NT = 8
TR = 64
TC = 512
LT = 128
HB = 24
WR = TR + 2 * HB
DIRS = [(-1, -1), (-1, 0), (-1, 1), (0, -1), (0, 1), (1, -1), (1, 0), (1, 1)]
ROWS = [(0, 0, 0, 112), (1, 4, 8, 96), (5, 7, 16, 80)]


def row_span(section):
    for first, last, start, rows in ROWS:
        if first <= section <= last:
            return start, rows


def roll(value, shift, axis):
    return pltpu.roll(value, shift % value.shape[axis], axis)


def kernel(
    gxn, gyn, u_ref, cond_ref, vel_ref, out_ref,
    ubuf, wbuf, xbuf, main, other, cwin, cedge, coef, fsend, frecv,
    load_sem, su, ru, sc, rc, sx, rx, sf, rf,
):
    ta = lax.axis_index("ta")
    gx = lax.axis_index("gx")
    gy = lax.axis_index("gy")
    even = lax.rem(ta, 2) == 0
    tile_m = ta // 2
    tile_o = lax.rem(tile_m + jnp.where(even, 3, 1), 4)

    def has(dx, dy):
        x, y = gx + dx, gy + dy
        return (x >= 0) & (x < gxn) & (y >= 0) & (y < gyn)

    lanes_m = pl.ds(pl.multiple_of(tile_m * LT, LT), LT)
    lanes_o = pl.ds(pl.multiple_of(tile_o * LT, LT), LT)
    loads = [
        pltpu.make_async_copy(u_ref.at[0], ubuf.at[pl.ds(HB, TR), pl.ds(0, TC)], load_sem.at[0]),
        pltpu.make_async_copy(cond_ref.at[:, lanes_m], main.at[0], load_sem.at[1]),
        pltpu.make_async_copy(cond_ref.at[:, lanes_o], other.at[0], load_sem.at[2]),
        pltpu.make_async_copy(vel_ref.at[:, :, lanes_m], main.at[pl.ds(1, 2)], load_sem.at[3]),
        pltpu.make_async_copy(vel_ref.at[:, :, lanes_o], other.at[pl.ds(1, 2)], load_sem.at[4]),
    ]
    for load in loads:
        load.start()

    ubuf[0:HB, :] = jnp.zeros((HB, 6 * LT), jnp.float32)
    ubuf[HB + TR : WR, :] = jnp.zeros((HB, 6 * LT), jnp.float32)
    ubuf[HB : HB + TR, TC:] = jnp.zeros((TR, 2 * LT), jnp.float32)
    cwin[:, 0:HB, :] = jnp.zeros((3, HB, LT), jnp.float32)
    cwin[:, HB + TR : WR, :] = jnp.zeros((3, HB, LT), jnp.float32)
    cedge[...] = jnp.zeros((3, WR, LT), jnp.float32)

    barrier = pltpu.get_barrier_semaphore()
    count = NT - 1
    for dx, dy in DIRS:
        near = has(dx, dy)
        count = count + near.astype(jnp.int32)

        @pl.when(near)
        def _():
            pl.semaphore_signal(barrier, inc=1, device_id=(ta, gx + dx, gy + dy), device_id_type=MESH)

    for step in range(1, NT):
        pl.semaphore_signal(
            barrier, inc=1, device_id=(lax.rem(ta + step, NT), gx, gy), device_id_type=MESH
        )
    for load in loads:
        load.wait()

    lane = lax.broadcasted_iota(jnp.int32, (TR, LT), 1)
    use_m = jnp.where(even, lane, LT - 1 - lane) < 96
    for part in range(3):
        cwin[part, HB : HB + TR, :] = jnp.where(use_m, main[part], other[part])
    pl.semaphore_wait(barrier, count)

    src_rows = {-1: pl.ds(0, HB), 0: pl.ds(0, TR), 1: pl.ds(TR - HB, HB)}
    dst_rows = {-1: pl.ds(HB + TR, HB), 0: pl.ds(HB, TR), 1: pl.ds(0, HB)}
    src_cols = {-1: pl.ds(0, LT), 0: pl.ds(0, TC), 1: pl.ds(TC - LT, LT)}
    dst_cols = {-1: pl.ds(TC, LT), 0: pl.ds(0, TC), 1: pl.ds(TC + LT, LT)}
    own_rows = {-1: pl.ds(HB, HB), 0: pl.ds(HB, TR), 1: pl.ds(TR, HB)}

    def state_copy(at):
        dx, dy = DIRS[at]
        return pltpu.make_async_remote_copy(
            src_ref=ubuf.at[own_rows[dx], src_cols[dy]],
            dst_ref=ubuf.at[dst_rows[dx], dst_cols[dy]],
            send_sem=su.at[at],
            recv_sem=ru.at[at],
            device_id=(ta, gx + dx, gy + dy),
            device_id_type=MESH,
        )

    def coef_copy(at):
        dx, dy = DIRS[at]
        if dy == 0:
            src, dst = cwin.at[:, own_rows[dx], :], cwin.at[:, dst_rows[dx], :]
        else:
            src, dst = other.at[:, src_rows[dx], :], cedge.at[:, dst_rows[dx], :]
        return pltpu.make_async_remote_copy(
            src_ref=src,
            dst_ref=dst,
            send_sem=sc.at[at],
            recv_sem=rc.at[at],
            device_id=(ta, gx + dx, gy + dy),
            device_id_type=MESH,
        )

    def coef_goes(dy):
        return {-1: ta == NT - 1, 0: ta >= 0, 1: ta == 0}[dy]

    for at, (dx, dy) in enumerate(DIRS):

        @pl.when(has(dx, dy))
        def _():
            state_copy(at).start()

    for at, (dx, dy) in enumerate(DIRS):

        @pl.when(has(dx, dy) & coef_goes(dy))
        def _():
            coef_copy(at).start()

    for at, (dx, dy) in enumerate(DIRS):

        @pl.when(has(-dx, -dy))
        def _():
            state_copy(at).wait_recv()

    wlane = lax.broadcasted_iota(jnp.int32, (WR, LT), 1)
    for owner in range(NT):
        tile = owner // 2
        if owner % 2 == 0:
            mate = tile - 1 if tile else 5
            keep = wlane < 96
        else:
            mate = tile + 1
            keep = wlane >= 32
        window = jnp.where(
            keep, ubuf[:, tile * LT : (tile + 1) * LT], ubuf[:, mate * LT : (mate + 1) * LT]
        )
        wbuf[owner] = window

    def window_copy(owner, span):
        start, rows = span
        return pltpu.make_async_remote_copy(
            src_ref=wbuf.at[owner, pl.ds(start, rows)],
            dst_ref=xbuf.at[ta, pl.ds(start, rows)],
            send_sem=sx.at[owner],
            recv_sem=rx.at[ta],
            device_id=(owner, gx, gy),
            device_id_type=MESH,
        )

    for first, last, start, rows in ROWS:

        @pl.when((ta >= first) & (ta <= last))
        def _():
            for step in range(1, NT):
                window_copy(lax.rem(ta + step, NT), (start, rows)).start()

    xbuf[ta] = wbuf[ta]

    for at, (dx, dy) in enumerate(DIRS):

        @pl.when(has(-dx, -dy) & coef_goes(dy))
        def _():
            coef_copy(at).wait_recv()

    row = lax.broadcasted_iota(jnp.int32, (WR, LT), 0)
    keep_m = jnp.where(even, wlane, LT - 1 - wlane) < 96
    take_edge = jnp.logical_not(keep_m) & ((ta == 0) | (ta == NT - 1))

    def mean(part):
        value = jnp.where(take_edge, cedge[part], cwin[part])
        value = value + roll(value, -1, 1)
        return value + roll(value, -1, 0)

    stiff = mean(0) * (0.25 * 0.1 / 6.0)
    vx = mean(1) * (0.25 * 0.1 / 8.0)
    vy = mean(2) * (0.25 * 0.1 / 8.0)
    gam = vx + vy
    kap = vx - vy
    column = (
        gy * TC + ta * 64 + jnp.where(
            even,
            jnp.where(wlane < 96, wlane, wlane - LT),
            jnp.where(wlane < 32, wlane + 64, wlane - 64),
        )
    )
    line = gx * TR + row - HB
    inside = (column >= 0) & (column < gyn * TC) & (line >= 0) & (line < gxn * TR)

    def put(slot, shift, value):
        coef[slot] = roll(jnp.where(inside, value, 0.0), shift, 0)

    def before(value):
        return roll(value, 1, 0)

    def left(value):
        return roll(value, 1, 1)

    put(0, 0, (4.0 * stiff - gam) + before(4.0 * stiff + kap) + left(4.0 * stiff - kap + before(4.0 * stiff + gam)))
    put(1, 0, (-stiff - kap) + before(gam - stiff))
    put(2, 0, left((-stiff - gam) + before(kap - stiff)))
    put(3, 1, (kap - stiff) + left(gam - stiff))
    put(4, 1, gam - 2.0 * stiff)
    put(5, 1, left(kap - 2.0 * stiff))
    put(6, -1, before((-stiff - gam) + left(-stiff - kap)))
    put(7, -1, before(-kap - 2.0 * stiff))
    put(8, -1, left(before(-gam - 2.0 * stiff)))

    def rate(value, span):
        start, rows = span
        high = roll(value, -1, 1)
        low = roll(value, 1, 1)

        def line_sum(slot):
            return (
                coef[slot, start : start + rows] * value
                + coef[slot + 1, start : start + rows] * high
                + coef[slot + 2, start : start + rows] * low
            )

        return line_sum(0) + roll(line_sum(3), -1, 0) + roll(line_sum(6), 1, 0)

    def trim(value, old, new):
        skip = new[0] - old[0]
        return value[skip : skip + new[1]]

    def result_copy(section):
        return pltpu.make_async_remote_copy(
            src_ref=fsend.at[section],
            dst_ref=frecv.at[ta],
            send_sem=sf.at[section],
            recv_sem=rf.at[ta],
            device_id=(section, gx, gy),
            device_id_type=MESH,
        )

    flane = lax.broadcasted_iota(jnp.int32, (TR // 2, LT), 1)
    fmain = jnp.where(even, flane, LT - 1 - flane) < 64
    state, state_span = None, None
    for section in range(NT):
        span = row_span(section)
        start, rows = span

        @pl.when(ta != section)
        def _():
            pltpu.make_async_remote_copy(
                src_ref=wbuf.at[section, pl.ds(start, rows)],
                dst_ref=xbuf.at[section, pl.ds(start, rows)],
                send_sem=sx.at[section],
                recv_sem=rx.at[section],
                device_id=(section, gx, gy),
                device_id_type=MESH,
            ).wait_recv()

        value = xbuf[section, start : start + rows]
        r1 = rate(value, span)
        r2 = rate(r1, span)
        r3 = rate(r2, span)
        r4 = rate(r3, span)
        delta = 0.25 * r4 - r3
        if section == 0:
            state, state_span = value - 2.0 * (r1 - r2) + delta, span
        else:
            now = row_span(section + 1 if section == 4 else section)
            state = trim(state, state_span, now)
            first = rate(state, now)
            second = rate(first, now)
            state = state - 2.0 * (first - second) + trim(delta, span, now)
            state_span = now
        tile = trim(state, state_span, (HB, TR))
        folded = jnp.where(fmain, tile[: TR // 2], roll(tile[TR // 2 :], 64, 1))
        fsend[section] = folded

        @pl.when(ta != section)
        def _():
            result_copy(section).start()

    frecv[ta] = fsend[ta]

    for step in range(1, NT):
        peer = lax.rem(ta + step, NT)
        pltpu.make_async_remote_copy(
            src_ref=fsend.at[peer],
            dst_ref=frecv.at[peer],
            send_sem=sf.at[peer],
            recv_sem=rf.at[peer],
            device_id=(peer, gx, gy),
            device_id_type=MESH,
        ).wait_recv()

    for tile in range(4):
        lower, upper = frecv[2 * tile], frecv[2 * tile + 1]
        lanes = slice(tile * LT, (tile + 1) * LT)
        out_ref[0, : TR // 2, lanes] = jnp.where(flane < 64, lower, upper)
        out_ref[0, TR // 2 :, lanes] = roll(jnp.where(flane < 64, upper, lower), 64, 1)

    for at, (dx, dy) in enumerate(DIRS):

        @pl.when(has(dx, dy))
        def _():
            state_copy(at).wait_send()

        @pl.when(has(dx, dy) & coef_goes(dy))
        def _():
            coef_copy(at).wait_send()

    for first, last, start, rows in ROWS:

        @pl.when((ta >= first) & (ta <= last))
        def _():
            for step in range(1, NT):
                window_copy(lax.rem(ta + step, NT), (start, rows)).wait_send()

    for step in range(1, NT):
        result_copy(lax.rem(ta + step, NT)).wait_send()


def solution(mesh):
    gxn, gyn = mesh.shape["gx"], mesh.shape["gy"]

    def local(start_states, conduct, velocity):
        return pl.pallas_call(
            functools.partial(kernel, gxn, gyn),
            out_shape=jax.ShapeDtypeStruct((1, TR, TC), jnp.float32),
            in_specs=[pl.BlockSpec(memory_space=pl.ANY)] * 3,
            out_specs=pl.BlockSpec(memory_space=pltpu.VMEM),
            scratch_shapes=[
                pltpu.VMEM((WR, 6 * LT), jnp.float32),
                pltpu.VMEM((NT, WR, LT), jnp.float32),
                pltpu.VMEM((NT, WR, LT), jnp.float32),
                pltpu.VMEM((3, TR, LT), jnp.float32),
                pltpu.VMEM((3, TR, LT), jnp.float32),
                pltpu.VMEM((3, WR, LT), jnp.float32),
                pltpu.VMEM((3, WR, LT), jnp.float32),
                pltpu.VMEM((9, WR, LT), jnp.float32),
                pltpu.VMEM((NT, TR // 2, LT), jnp.float32),
                pltpu.VMEM((NT, TR // 2, LT), jnp.float32),
                pltpu.SemaphoreType.DMA((5,)),
            ]
            + [pltpu.SemaphoreType.DMA((8,))] * 8,
            compiler_params=pltpu.CompilerParams(
                collective_id=0, has_side_effects=True
            ),
        )(start_states, conduct, velocity)

    in_specs = (P("ta", "gx", "gy"), P("gx", "gy"), P(None, "gx", "gy"))
    return jax.shard_map(
        local, mesh=mesh, in_specs=in_specs, out_specs=P("ta", "gx", "gy"), check_vma=False
    )
```

```python
import functools

import jax
import jax.numpy as jnp
from jax import lax
from jax.experimental import pallas as pl
from jax.experimental.pallas import tpu as pltpu
from jax.sharding import PartitionSpec as P

MESH = pl.DeviceIdType.MESH
NT = 8
TR = 64
TC = 512
LT = 128
HB = 24
WR = TR + 2 * HB
ER = 32
ROWS = [(0, 0, 0, 112), (1, 4, 8, 96), (5, 7, 16, 80)]
SPANS = [(0, 112), (8, 96), (8, 96), (8, 96), (16, 80), (16, 80), (16, 80), (16, 80)]
EDGE = {1: (0, 8), 0: (8, 16), -1: (24, 8)}


def row_span(section):
    for first, last, start, rows in ROWS:
        if first <= section <= last:
            return start, rows


def roll(value, shift, axis):
    return pltpu.roll(value, shift % value.shape[axis], axis)


def fold(read, base):
    lane = lax.broadcasted_iota(jnp.int32, (8, LT), 1)
    parts = []
    for start, groups in ((40, 3), (0, 4), (32, 4), (0, 3)):
        value = roll(read(start), base, 1)
        for group in range(1, groups):
            moved = roll(read(start + 8 * group), base + 32 * group, 1)
            value = jnp.where(lane < 32 * group, value, moved)
        parts.append(value)
    return parts


def unfold(read, base):
    for start, groups, first in ((0, 3, 0), (8, 4, 3), (16, 4, 7), (24, 3, 11)):
        value = read(start)
        for group in range(groups):
            yield first + group, roll(value, base - 32 * group, 1)


def kernel(
    gxn, gyn, u_ref, cond_ref, vel_ref, out_ref,
    ubuf, wbuf, xbuf, ebuf, xedge, main, other, cwin, cfull, cfold, cedge, coef, fsend, frecv,
    load_sem, s_main, r_main, s_strip, r_strip, s_edge, r_edge, sc, rc, sf, rf,
):
    ta = lax.axis_index("ta")
    gx = lax.axis_index("gx")
    gy = lax.axis_index("gy")
    even = lax.rem(ta, 2) == 0
    tile_m = ta // 2
    tile_o = lax.rem(tile_m + jnp.where(even, 3, 1), 4)

    def has(dx, dy):
        x, y = gx + dx, gy + dy
        return (x >= 0) & (x < gxn) & (y >= 0) & (y < gyn)

    def ring(step):
        return lax.rem(ta + step, NT)

    lanes_m = pl.ds(pl.multiple_of(tile_m * LT, LT), LT)
    lanes_o = pl.ds(pl.multiple_of(tile_o * LT, LT), LT)
    loads = [
        pltpu.make_async_copy(u_ref.at[0], ubuf, load_sem.at[0]),
        pltpu.make_async_copy(cond_ref.at[:, lanes_m], main.at[0], load_sem.at[1]),
        pltpu.make_async_copy(cond_ref.at[:, lanes_o], other.at[0], load_sem.at[2]),
        pltpu.make_async_copy(vel_ref.at[:, :, lanes_m], main.at[pl.ds(1, 2)], load_sem.at[3]),
        pltpu.make_async_copy(vel_ref.at[:, :, lanes_o], other.at[pl.ds(1, 2)], load_sem.at[4]),
    ]
    for load in loads:
        load.start()

    xbuf[:, 0:HB, :] = jnp.zeros((NT, HB, LT), jnp.float32)
    xbuf[:, HB + TR : WR, :] = jnp.zeros((NT, HB, LT), jnp.float32)
    xedge[...] = jnp.zeros((NT, ER, LT), jnp.float32)
    cwin[:, 0:HB, :] = jnp.zeros((3, HB, LT), jnp.float32)
    cwin[:, HB + TR : WR, :] = jnp.zeros((3, HB, LT), jnp.float32)
    cedge[...] = jnp.zeros((3, ER, LT), jnp.float32)

    barrier = pltpu.get_barrier_semaphore()

    def greet(section, dx, dy):
        pl.semaphore_signal(
            barrier, inc=1, device_id=(section, gx + dx, gy + dy), device_id_type=MESH
        )

    for dx in (-1, 1):

        @pl.when(has(dx, 0))
        def _():
            for step in range(NT):
                greet(ring(step), dx, 0)

    for owner, dy in ((0, -1), (NT - 1, 1)):
        for dx in (-1, 0, 1):

            @pl.when((ta == owner) & has(dx, dy))
            def _():
                for step in range(NT):
                    greet(ring(step), dx, dy)

    for step in range(1, NT):
        greet(ring(step), 0, 0)

    count = NT - 1
    for dx in (-1, 1):
        count = count + NT * has(dx, 0).astype(jnp.int32)
    for dy in (-1, 1):
        for dx in (-1, 0, 1):
            count = count + has(dx, dy).astype(jnp.int32)

    for load in loads:
        load.wait()

    lane = lax.broadcasted_iota(jnp.int32, (TR, LT), 1)
    for owner in range(NT):
        tile = owner // 2
        if owner % 2 == 0:
            mate, keep = (tile + 3) % 4, lane < 96
        else:
            mate, keep = (tile + 1) % 4, lane >= 32
        wbuf[owner] = jnp.where(
            keep, ubuf[:, tile * LT : (tile + 1) * LT], ubuf[:, mate * LT : (mate + 1) * LT]
        )
    for slot, (first, base) in enumerate(((3 * LT, 32), (0, 0))):
        for at, part in enumerate(fold(lambda start: ubuf[start : start + 8, first : first + LT], base)):
            ebuf[slot, 8 * at : 8 * at + 8] = part
    use_m = jnp.where(even, lane, LT - 1 - lane) < 96
    for part in range(3):
        cwin[part, HB : HB + TR, :] = jnp.where(use_m, main[part], other[part])
    for owner, base in ((0, 32), (NT - 1, 0)):

        @pl.when(ta == owner)
        def _():
            for part in range(3):
                for at, value in enumerate(fold(lambda start: other[part, start : start + 8], base)):
                    cfold[part, 8 * at : 8 * at + 8] = value

    xbuf[ta, HB : HB + TR] = wbuf[ta]
    pl.semaphore_wait(barrier, count)

    def main_copy(owner, section):
        return pltpu.make_async_remote_copy(
            src_ref=wbuf.at[owner],
            dst_ref=xbuf.at[section, pl.ds(HB, TR)],
            send_sem=s_main.at[owner],
            recv_sem=r_main.at[section],
            device_id=(owner, gx, gy),
            device_id_type=MESH,
        )

    def strip_copy(owner, section, dx, rows, here=False):
        if dx < 0:
            src, dst = pl.ds(0, rows), pl.ds(HB + TR, rows)
        else:
            src, dst = pl.ds(TR - rows, rows), pl.ds(HB - rows, rows)
        side = (dx + 1) // 2
        return pltpu.make_async_remote_copy(
            src_ref=wbuf.at[owner, src],
            dst_ref=xbuf.at[section, dst],
            send_sem=s_strip.at[NT * side + owner],
            recv_sem=r_strip.at[NT * side + section],
            device_id=(ta, gx, gy) if here else (owner, gx + dx, gy),
            device_id_type=MESH,
        )

    def edge_copy(section, dx, dy, here=False):
        slot, owner = (0, 0) if dy > 0 else (1, NT - 1)
        start, rows = EDGE[dx]
        return pltpu.make_async_remote_copy(
            src_ref=ebuf.at[slot, pl.ds(start, rows)],
            dst_ref=xedge.at[section, pl.ds(start, rows)],
            send_sem=s_edge.at[3 * slot + dx + 1],
            recv_sem=r_edge.at[3 * section + dx + 1],
            device_id=(ta, gx, gy) if here else (ring(lax.rem(owner + NT - ta, NT)), gx + dx, gy + dy),
            device_id_type=MESH,
        )

    def coef_copy(dx, dy, here=False):
        if dy == 0:
            if dx < 0:
                src, dst = pl.ds(HB, HB), pl.ds(HB + TR, HB)
            else:
                src, dst = pl.ds(TR, HB), pl.ds(0, HB)
            src, dst = cwin.at[:, src, :], cwin.at[:, dst, :]
        else:
            place = pl.ds(*EDGE[dx])
            src, dst = cfold.at[:, place, :], cedge.at[:, place, :]
        at = 3 * (1 if dy else 0) + dx + 1
        return pltpu.make_async_remote_copy(
            src_ref=src,
            dst_ref=dst,
            send_sem=sc.at[at],
            recv_sem=rc.at[at],
            device_id=(ta, gx, gy) if here else (ta, gx + dx, gy + dy),
            device_id_type=MESH,
        )

    coef_dirs = [(-1, 0, None), (1, 0, None)]
    coef_dirs += [(dx, 1, 0) for dx in (-1, 0, 1)] + [(dx, -1, NT - 1) for dx in (-1, 0, 1)]

    def sends(act):
        for dx, dy, only in coef_dirs:
            near = has(dx, dy)

            @pl.when(near if only is None else near & (ta == only))
            def _():
                act(coef_copy(dx, dy))

        for first, last, _, rows in ROWS:

            @pl.when((ta >= first) & (ta <= last))
            def _():
                for dx in (-1, 1):

                    @pl.when(has(dx, 0))
                    def _():
                        for step in range(NT):
                            act(strip_copy(ring(step), ta, dx, (rows - TR) // 2))

        for step in range(1, NT):
            act(main_copy(ring(step), ta))
        for dy in (-1, 1):
            for dx in (-1, 0, 1):

                @pl.when(has(dx, dy))
                def _():
                    act(edge_copy(ta, dx, dy))

    sends(lambda copy: copy.start())

    for dx, dy, only in coef_dirs:
        near = has(-dx, -dy)

        @pl.when(near if only is None else near & (ta == only))
        def _():
            coef_copy(dx, dy, True).wait_recv()

    cfull[...] = cwin[...]
    edge_lane = lax.broadcasted_iota(jnp.int32, (8, LT), 1)
    for owner, base in ((0, 96), (NT - 1, 0)):

        @pl.when(ta == owner)
        def _():
            mine = (edge_lane >= base) & (edge_lane < base + 32)
            for part in range(3):
                for at, value in unfold(lambda start: cedge[part, start : start + 8], base):
                    rows = slice(8 * at, 8 * at + 8)
                    cfull[part, rows] = jnp.where(mine, value, cfull[part, rows])

    wlane = lax.broadcasted_iota(jnp.int32, (WR, LT), 1)
    row = lax.broadcasted_iota(jnp.int32, (WR, LT), 0)

    def mean(part):
        value = cfull[part]
        value = value + roll(value, -1, 1)
        return value + roll(value, -1, 0)

    stiff = mean(0) * (0.25 * 0.1 / 6.0)
    vx = mean(1) * (0.25 * 0.1 / 8.0)
    vy = mean(2) * (0.25 * 0.1 / 8.0)
    gam = vx + vy
    kap = vx - vy
    column = (
        gy * TC + ta * 64 + jnp.where(
            even,
            jnp.where(wlane < 96, wlane, wlane - LT),
            jnp.where(wlane < 32, wlane + 64, wlane - 64),
        )
    )
    line = gx * TR + row - HB
    inside = (column >= 0) & (column < gyn * TC) & (line >= 0) & (line < gxn * TR)

    def put(slot, shift, value):
        coef[slot] = roll(jnp.where(inside, value, 0.0), shift, 0)

    def before(value):
        return roll(value, 1, 0)

    def left(value):
        return roll(value, 1, 1)

    put(0, 0, (4.0 * stiff - gam) + before(4.0 * stiff + kap) + left(4.0 * stiff - kap + before(4.0 * stiff + gam)))
    put(1, 0, (-stiff - kap) + before(gam - stiff))
    put(2, 0, left((-stiff - gam) + before(kap - stiff)))
    put(3, 1, (kap - stiff) + left(gam - stiff))
    put(4, 1, gam - 2.0 * stiff)
    put(5, 1, left(kap - 2.0 * stiff))
    put(6, -1, before((-stiff - gam) + left(-stiff - kap)))
    put(7, -1, before(-kap - 2.0 * stiff))
    put(8, -1, left(before(-gam - 2.0 * stiff)))

    def rate(value, span):
        start, rows = span
        high = roll(value, -1, 1)
        low = roll(value, 1, 1)

        def line_sum(slot):
            return (
                coef[slot, start : start + rows] * value
                + coef[slot + 1, start : start + rows] * high
                + coef[slot + 2, start : start + rows] * low
            )

        return line_sum(0) + roll(line_sum(3), -1, 0) + roll(line_sum(6), 1, 0)

    def trim(value, old, new):
        skip = new[0] - old[0]
        return value[skip : skip + new[1]]

    def result_copy(section):
        return pltpu.make_async_remote_copy(
            src_ref=fsend.at[section],
            dst_ref=frecv.at[ta],
            send_sem=sf.at[section],
            recv_sem=rf.at[ta],
            device_id=(section, gx, gy),
            device_id_type=MESH,
        )

    flane = lax.broadcasted_iota(jnp.int32, (TR // 2, LT), 1)
    fmain = jnp.where(even, flane, LT - 1 - flane) < 64
    def arrive(section):
        span = row_span(section)
        start, rows = span
        @pl.when(ta != section)
        def _():
            main_copy(section, section).wait_recv()

        for dx in (-1, 1):

            @pl.when(has(-dx, 0))
            def _():
                strip_copy(section, section, dx, (rows - TR) // 2, True).wait_recv()

        for owner, dy, base in ((0, 1, 96), (NT - 1, -1, 0)):

            @pl.when(ta == owner)
            def _():
                for dx in (-1, 0, 1):

                    @pl.when(has(-dx, -dy))
                    def _():
                        edge_copy(section, dx, dy, True).wait_recv()

                mine = (edge_lane >= base) & (edge_lane < base + 32)
                for at, value in unfold(lambda start: xedge[section, start : start + 8], base):
                    place = slice(8 * at, 8 * at + 8)
                    xbuf[section, place] = jnp.where(mine, value, xbuf[section, place])

        value = xbuf[section, start : start + rows]
        return value, 0.5 * rate(value - 0.25 * rate(value, span), span), span

    def advance(state, state_span, half, half_span, span):
        state = trim(state, state_span, span)
        inner = state - trim(half, half_span, span)
        return state - 2.0 * rate(state - rate(inner, span), span)

    def give(section, state, span):
        tile = trim(state, span, (HB, TR))
        folded = jnp.where(fmain, tile[: TR // 2], roll(tile[TR // 2 :], 64, 1))
        fsend[section] = folded

        @pl.when(ta != section)
        def _():
            result_copy(section).start()

    state, half, span = arrive(0)
    half_span = span
    for section in range(NT):
        after = arrive(section + 1) if section + 1 < NT else None
        now = SPANS[section]
        state = advance(state, span, half, half_span, now)
        span = now
        give(section, state, span)
        if after is not None:
            half, half_span = after[1], after[2]

    frecv[ta] = fsend[ta]

    for step in range(1, NT):
        peer = lax.rem(ta + step, NT)
        pltpu.make_async_remote_copy(
            src_ref=fsend.at[peer],
            dst_ref=frecv.at[peer],
            send_sem=sf.at[peer],
            recv_sem=rf.at[peer],
            device_id=(peer, gx, gy),
            device_id_type=MESH,
        ).wait_recv()

    for tile in range(4):
        lower, upper = frecv[2 * tile], frecv[2 * tile + 1]
        lanes = slice(tile * LT, (tile + 1) * LT)
        out_ref[0, : TR // 2, lanes] = jnp.where(flane < 64, lower, upper)
        out_ref[0, TR // 2 :, lanes] = roll(jnp.where(flane < 64, upper, lower), 64, 1)

    sends(lambda copy: copy.wait_send())
    for step in range(1, NT):
        result_copy(lax.rem(ta + step, NT)).wait_send()


def solution(mesh):
    gxn, gyn = mesh.shape["gx"], mesh.shape["gy"]

    def local(start_states, conduct, velocity):
        return pl.pallas_call(
            functools.partial(kernel, gxn, gyn),
            out_shape=pltpu.VMEM((1, TR, TC), jnp.float32),
            in_specs=[pl.BlockSpec(memory_space=pl.ANY)] * 3,
            out_specs=pl.BlockSpec(memory_space=pltpu.VMEM),
            scratch_shapes=[
                pltpu.VMEM((TR, TC), jnp.float32),
                pltpu.VMEM((NT, TR, LT), jnp.float32),
                pltpu.VMEM((NT, WR, LT), jnp.float32),
                pltpu.VMEM((2, ER, LT), jnp.float32),
                pltpu.VMEM((NT, ER, LT), jnp.float32),
                pltpu.VMEM((3, TR, LT), jnp.float32),
                pltpu.VMEM((3, TR, LT), jnp.float32),
                pltpu.VMEM((3, WR, LT), jnp.float32),
                pltpu.VMEM((3, WR, LT), jnp.float32),
                pltpu.VMEM((3, ER, LT), jnp.float32),
                pltpu.VMEM((3, ER, LT), jnp.float32),
                pltpu.VMEM((9, WR, LT), jnp.float32),
                pltpu.VMEM((NT, TR // 2, LT), jnp.float32),
                pltpu.VMEM((NT, TR // 2, LT), jnp.float32),
                pltpu.SemaphoreType.DMA((5,)),
                pltpu.SemaphoreType.DMA((NT,)),
                pltpu.SemaphoreType.DMA((NT,)),
                pltpu.SemaphoreType.DMA((2 * NT,)),
                pltpu.SemaphoreType.DMA((2 * NT,)),
                pltpu.SemaphoreType.DMA((6,)),
                pltpu.SemaphoreType.DMA((3 * NT,)),
                pltpu.SemaphoreType.DMA((6,)),
                pltpu.SemaphoreType.DMA((6,)),
                pltpu.SemaphoreType.DMA((NT,)),
                pltpu.SemaphoreType.DMA((NT,)),
            ],
            compiler_params=pltpu.CompilerParams(collective_id=0, has_side_effects=True),
        )(start_states, conduct, velocity)

    in_specs = (P("ta", "gx", "gy"), P("gx", "gy"), P(None, "gx", "gy"))
    return jax.shard_map(
        local, mesh=mesh, in_specs=in_specs, out_specs=P("ta", "gx", "gy"), check_vma=False
    )
```

```python
import functools

import jax
import jax.numpy as jnp
from jax import lax
from jax.experimental import pallas as pl
from jax.experimental.pallas import tpu as pltpu
from jax.sharding import PartitionSpec as P

MESH = pl.DeviceIdType.MESH
NT = 8
TR = 64
TC = 512
LT = 128
HB = 24
WR = TR + 2 * HB
ER = 32
ROWS = [(0, 0, 24), (1, 7, 16)]
FULL = (0, WR)
SPAN = (8, WR - 16)
LAST = (16, WR - 32)
EDGE = {1: (0, 8), 0: (8, 16), -1: (24, 8)}


def roll(value, shift, axis):
    return pltpu.roll(value, shift % value.shape[axis], axis)


def fold(read, base):
    lane = lax.broadcasted_iota(jnp.int32, (8, LT), 1)
    parts = []
    for start, groups in ((40, 3), (0, 4), (32, 4), (0, 3)):
        value = roll(read(start), base, 1)
        for group in range(1, groups):
            moved = roll(read(start + 8 * group), base + 32 * group, 1)
            value = jnp.where(lane < 32 * group, value, moved)
        parts.append(value)
    return parts


def unfold(read, base):
    for start, groups, first in ((0, 3, 0), (8, 4, 3), (16, 4, 7), (24, 3, 11)):
        value = read(start)
        for group in range(groups):
            yield first + group, roll(value, base - 32 * group, 1)


def kernel(
    gxn, gyn, u_ref, cond_ref, vel_ref, out_ref,
    ubuf, wbuf, xbuf, ebuf, xedge, main, other, cwin, cfull, cfold, cedge, coef, state, half, fsend, frecv,
    load_sem, s_main, r_main, s_strip, r_strip, s_edge, r_edge, sc, rc, sf, rf,
):
    ta = lax.axis_index("ta")
    gx = lax.axis_index("gx")
    gy = lax.axis_index("gy")
    even = lax.rem(ta, 2) == 0
    tile_m = ta // 2
    tile_o = lax.rem(tile_m + jnp.where(even, 3, 1), 4)

    def has(dx, dy):
        x, y = gx + dx, gy + dy
        return (x >= 0) & (x < gxn) & (y >= 0) & (y < gyn)

    def ring(step):
        return lax.rem(ta + step, NT)

    barrier = pltpu.get_barrier_semaphore()

    def greet(section, dx, dy):
        pl.semaphore_signal(
            barrier, inc=1, device_id=(section, gx + dx, gy + dy), device_id_type=MESH
        )

    for dx in (-1, 1):

        @pl.when(has(dx, 0))
        def _():
            for step in range(NT):
                greet(ring(step), dx, 0)

    for owner, dy in ((0, -1), (NT - 1, 1)):
        for dx in (-1, 0, 1):

            @pl.when((ta == owner) & has(dx, dy))
            def _():
                for step in range(NT):
                    greet(ring(step), dx, dy)

    for step in range(1, NT):
        greet(ring(step), 0, 0)

    lanes_m = pl.ds(pl.multiple_of(tile_m * LT, LT), LT)
    lanes_o = pl.ds(pl.multiple_of(tile_o * LT, LT), LT)
    loads = [
        pltpu.make_async_copy(u_ref.at[0], ubuf, load_sem.at[0]),
        pltpu.make_async_copy(cond_ref.at[:, lanes_m], main.at[0], load_sem.at[1]),
        pltpu.make_async_copy(cond_ref.at[:, lanes_o], other.at[0], load_sem.at[2]),
        pltpu.make_async_copy(vel_ref.at[:, :, lanes_m], main.at[pl.ds(1, 2)], load_sem.at[3]),
        pltpu.make_async_copy(vel_ref.at[:, :, lanes_o], other.at[pl.ds(1, 2)], load_sem.at[4]),
    ]
    for load in loads:
        load.start()

    count = NT - 1
    for dx in (-1, 1):
        count = count + NT * has(dx, 0).astype(jnp.int32)
    for dy in (-1, 1):
        for dx in (-1, 0, 1):
            count = count + has(dx, dy).astype(jnp.int32)

    def clear(ref, planes, start, rows):
        ref[:, start : start + rows, :] = jnp.zeros((planes, rows, LT), jnp.float32)

    for dx, start in ((1, 0), (-1, HB + TR)):

        @pl.when(jnp.logical_not(has(-dx, 0)))
        def _():
            clear(xbuf, NT, start, HB)
            clear(cwin, 3, start, HB)

    for owner, dy in ((0, 1), (NT - 1, -1)):
        for dx in (-1, 0, 1):

            @pl.when((ta == owner) & jnp.logical_not(has(-dx, -dy)))
            def _():
                clear(xedge, NT, *EDGE[dx])
                clear(cedge, 3, *EDGE[dx])

    for load in loads:
        load.wait()

    lane = lax.broadcasted_iota(jnp.int32, (TR, LT), 1)
    for owner in range(NT):
        tile = owner // 2
        if owner % 2 == 0:
            mate, keep = (tile + 3) % 4, lane < 96
        else:
            mate, keep = (tile + 1) % 4, lane >= 32
        wbuf[owner] = jnp.where(
            keep, ubuf[:, tile * LT : (tile + 1) * LT], ubuf[:, mate * LT : (mate + 1) * LT]
        )
    for slot, (first, base) in enumerate(((3 * LT, 32), (0, 0))):
        for at, part in enumerate(fold(lambda start: ubuf[start : start + 8, first : first + LT], base)):
            ebuf[slot, 8 * at : 8 * at + 8] = part
    use_m = jnp.where(even, lane, LT - 1 - lane) < 96
    for part in range(3):
        cwin[part, HB : HB + TR, :] = jnp.where(use_m, main[part], other[part])
    for owner, base in ((0, 32), (NT - 1, 0)):

        @pl.when(ta == owner)
        def _():
            for part in range(3):
                for at, value in enumerate(fold(lambda start: other[part, start : start + 8], base)):
                    cfold[part, 8 * at : 8 * at + 8] = value

    xbuf[ta, HB : HB + TR] = wbuf[ta]
    pl.semaphore_wait(barrier, count)

    def main_copy(owner, section):
        return pltpu.make_async_remote_copy(
            src_ref=wbuf.at[owner],
            dst_ref=xbuf.at[section, pl.ds(HB, TR)],
            send_sem=s_main.at[owner],
            recv_sem=r_main.at[section],
            device_id=(owner, gx, gy),
            device_id_type=MESH,
        )

    def strip_copy(owner, section, dx, rows, here=False):
        if dx < 0:
            src, dst = pl.ds(0, rows), pl.ds(HB + TR, rows)
        else:
            src, dst = pl.ds(TR - rows, rows), pl.ds(HB - rows, rows)
        side = (dx + 1) // 2
        return pltpu.make_async_remote_copy(
            src_ref=wbuf.at[owner, src],
            dst_ref=xbuf.at[section, dst],
            send_sem=s_strip.at[NT * side + owner],
            recv_sem=r_strip.at[NT * side + section],
            device_id=(ta, gx, gy) if here else (owner, gx + dx, gy),
            device_id_type=MESH,
        )

    def edge_copy(section, dx, dy, here=False):
        slot, owner = (0, 0) if dy > 0 else (1, NT - 1)
        start, rows = EDGE[dx]
        return pltpu.make_async_remote_copy(
            src_ref=ebuf.at[slot, pl.ds(start, rows)],
            dst_ref=xedge.at[section, pl.ds(start, rows)],
            send_sem=s_edge.at[3 * slot + dx + 1],
            recv_sem=r_edge.at[3 * section + dx + 1],
            device_id=(ta, gx, gy) if here else (ring(lax.rem(owner + NT - ta, NT)), gx + dx, gy + dy),
            device_id_type=MESH,
        )

    def coef_copy(dx, dy, here=False):
        if dy == 0:
            if dx < 0:
                src, dst = pl.ds(HB, HB), pl.ds(HB + TR, HB)
            else:
                src, dst = pl.ds(TR, HB), pl.ds(0, HB)
            src, dst = cwin.at[:, src, :], cwin.at[:, dst, :]
        else:
            place = pl.ds(*EDGE[dx])
            src, dst = cfold.at[:, place, :], cedge.at[:, place, :]
        at = 3 * (1 if dy else 0) + dx + 1
        return pltpu.make_async_remote_copy(
            src_ref=src,
            dst_ref=dst,
            send_sem=sc.at[at],
            recv_sem=rc.at[at],
            device_id=(ta, gx, gy) if here else (ta, gx + dx, gy + dy),
            device_id_type=MESH,
        )

    coef_dirs = [(-1, 0, None), (1, 0, None)]
    coef_dirs += [(dx, 1, 0) for dx in (-1, 0, 1)] + [(dx, -1, NT - 1) for dx in (-1, 0, 1)]

    def sends(act):
        for dx in (-1, 1, 0):
            for dy in (-1, 1):

                @pl.when(has(dx, dy))
                def _():
                    act(edge_copy(ta, dx, dy))

        for dx, dy, only in coef_dirs:
            near = has(dx, dy)

            @pl.when(near if only is None else near & (ta == only))
            def _():
                act(coef_copy(dx, dy))

        for first, last, rows in ROWS:

            @pl.when((ta >= first) & (ta <= last))
            def _():
                for dx in (-1, 1):

                    @pl.when(has(dx, 0))
                    def _():
                        for step in range(NT):
                            act(strip_copy(ring(step), ta, dx, rows))

        for step in range(1, NT):
            act(main_copy(ring(step), ta))

    sends(lambda copy: copy.start())

    for dx, dy, only in coef_dirs:
        near = has(-dx, -dy)

        @pl.when(near if only is None else near & (ta == only))
        def _():
            coef_copy(dx, dy, True).wait_recv()

    cfull[...] = cwin[...]
    edge_lane = lax.broadcasted_iota(jnp.int32, (8, LT), 1)
    for owner, base in ((0, 96), (NT - 1, 0)):

        @pl.when(ta == owner)
        def _():
            mine = (edge_lane >= base) & (edge_lane < base + 32)
            for part in range(3):
                for at, value in unfold(lambda start: cedge[part, start : start + 8], base):
                    rows = slice(8 * at, 8 * at + 8)
                    cfull[part, rows] = jnp.where(mine, value, cfull[part, rows])

    wlane = lax.broadcasted_iota(jnp.int32, (WR, LT), 1)
    row = lax.broadcasted_iota(jnp.int32, (WR, LT), 0)

    def mean(part):
        value = cfull[part]
        value = value + roll(value, -1, 1)
        return value + roll(value, -1, 0)

    stiff = mean(0) * (0.25 * 0.1 / 6.0)
    vx = mean(1) * (0.25 * 0.1 / 8.0)
    vy = mean(2) * (0.25 * 0.1 / 8.0)
    gam = vx + vy
    kap = vx - vy
    column = (
        gy * TC + ta * 64 + jnp.where(
            even,
            jnp.where(wlane < 96, wlane, wlane - LT),
            jnp.where(wlane < 32, wlane + 64, wlane - 64),
        )
    )
    line = gx * TR + row - HB
    inside = (column >= 0) & (column < gyn * TC) & (line >= 0) & (line < gxn * TR)

    def put(slot, shift, value):
        coef[slot] = roll(jnp.where(inside, value, 0.0), shift, 0)

    def before(value):
        return roll(value, 1, 0)

    def left(value):
        return roll(value, 1, 1)

    put(0, 0, (4.0 * stiff - gam) + before(4.0 * stiff + kap) + left(4.0 * stiff - kap + before(4.0 * stiff + gam)))
    put(1, 0, (-stiff - kap) + before(gam - stiff))
    put(2, 0, left((-stiff - gam) + before(kap - stiff)))
    put(3, 1, (kap - stiff) + left(gam - stiff))
    put(4, 1, gam - 2.0 * stiff)
    put(5, 1, left(kap - 2.0 * stiff))
    put(6, -1, before((-stiff - gam) + left(-stiff - kap)))
    put(7, -1, before(-kap - 2.0 * stiff))
    put(8, -1, left(before(-gam - 2.0 * stiff)))

    def rate(value, span):
        start, rows = span
        high = roll(value, -1, 1)
        low = roll(value, 1, 1)

        def line_sum(slot):
            return (
                coef[slot, start : start + rows] * value
                + coef[slot + 1, start : start + rows] * high
                + coef[slot + 2, start : start + rows] * low
            )

        return line_sum(0) + roll(line_sum(3), -1, 0) + roll(line_sum(6), 1, 0)

    def trim(value, old, new):
        skip = new[0] - old[0]
        return value[skip : skip + new[1]]

    def result_copy(section):
        return pltpu.make_async_remote_copy(
            src_ref=fsend.at[section],
            dst_ref=frecv.at[ta],
            send_sem=sf.at[section],
            recv_sem=rf.at[ta],
            device_id=(section, gx, gy),
            device_id_type=MESH,
        )

    flane = lax.broadcasted_iota(jnp.int32, (TR // 2, LT), 1)
    fmain = jnp.where(even, flane, LT - 1 - flane) < 64
    def arrive(section, halo, span):
        @pl.when(ta != section)
        def _():
            main_copy(section, section).wait_recv()

        for dx in (-1, 1):

            @pl.when(has(-dx, 0))
            def _():
                strip_copy(section, section, dx, halo, True).wait_recv()

        for owner, dy, base in ((0, 1, 96), (NT - 1, -1, 0)):

            @pl.when(ta == owner)
            def _():
                for dx in (-1, 0, 1):

                    @pl.when(has(-dx, -dy))
                    def _():
                        edge_copy(section, dx, dy, True).wait_recv()

                mine = (edge_lane >= base) & (edge_lane < base + 32)
                for at, value in unfold(lambda start: xedge[section, start : start + 8], base):
                    if span[0] <= 8 * at < span[0] + span[1]:
                        place = slice(8 * at, 8 * at + 8)
                        xbuf[section, place] = jnp.where(mine, value, xbuf[section, place])

        value = xbuf[section, span[0] : span[0] + span[1]]
        return 0.5 * rate(value - 0.25 * rate(value, span), span)

    def advance(value, half, span):
        return value - 2.0 * rate(value - rate(value - half, span), span)

    def give(section, value, span):
        tile = trim(value, span, (HB, TR))
        fsend[section] = jnp.where(fmain, tile[: TR // 2], roll(tile[TR // 2 :], 64, 1))

        @pl.when(ta != section)
        def _():
            result_copy(section).start()

    inner = slice(SPAN[0], SPAN[0] + SPAN[1])
    last = slice(LAST[0], LAST[0] + LAST[1])
    half[...] = arrive(0, HB, FULL)
    state[inner] = xbuf[0, inner]

    def step(section, carry):
        after = arrive(section, 16, SPAN)
        value = advance(state[inner], half[inner], SPAN)
        state[inner] = value
        half[inner] = after
        give(section - 1, value, SPAN)
        return carry

    lax.fori_loop(1, NT, step, 0)
    give(NT - 1, advance(state[last], half[last], LAST), LAST)

    frecv[ta] = fsend[ta]

    for step in range(1, NT):
        peer = lax.rem(ta + step, NT)
        pltpu.make_async_remote_copy(
            src_ref=fsend.at[peer],
            dst_ref=frecv.at[peer],
            send_sem=sf.at[peer],
            recv_sem=rf.at[peer],
            device_id=(peer, gx, gy),
            device_id_type=MESH,
        ).wait_recv()

    for tile in range(4):
        lower, upper = frecv[2 * tile], frecv[2 * tile + 1]
        lanes = slice(tile * LT, (tile + 1) * LT)
        out_ref[0, : TR // 2, lanes] = jnp.where(flane < 64, lower, upper)
        out_ref[0, TR // 2 :, lanes] = roll(jnp.where(flane < 64, upper, lower), 64, 1)

    sends(lambda copy: copy.wait_send())
    for step in range(1, NT):
        result_copy(lax.rem(ta + step, NT)).wait_send()


def solution(mesh):
    gxn, gyn = mesh.shape["gx"], mesh.shape["gy"]

    def local(start_states, conduct, velocity):
        return pl.pallas_call(
            functools.partial(kernel, gxn, gyn),
            out_shape=pltpu.VMEM((1, TR, TC), jnp.float32),
            in_specs=[pl.BlockSpec(memory_space=pl.ANY)] * 3,
            out_specs=pl.BlockSpec(memory_space=pltpu.VMEM),
            scratch_shapes=[
                pltpu.VMEM((TR, TC), jnp.float32),
                pltpu.VMEM((NT, TR, LT), jnp.float32),
                pltpu.VMEM((NT, WR, LT), jnp.float32),
                pltpu.VMEM((2, ER, LT), jnp.float32),
                pltpu.VMEM((NT, ER, LT), jnp.float32),
                pltpu.VMEM((3, TR, LT), jnp.float32),
                pltpu.VMEM((3, TR, LT), jnp.float32),
                pltpu.VMEM((3, WR, LT), jnp.float32),
                pltpu.VMEM((3, WR, LT), jnp.float32),
                pltpu.VMEM((3, ER, LT), jnp.float32),
                pltpu.VMEM((3, ER, LT), jnp.float32),
                pltpu.VMEM((9, WR, LT), jnp.float32),
                pltpu.VMEM((WR, LT), jnp.float32),
                pltpu.VMEM((WR, LT), jnp.float32),
                pltpu.VMEM((NT, TR // 2, LT), jnp.float32),
                pltpu.VMEM((NT, TR // 2, LT), jnp.float32),
                pltpu.SemaphoreType.DMA((5,)),
                pltpu.SemaphoreType.DMA((NT,)),
                pltpu.SemaphoreType.DMA((NT,)),
                pltpu.SemaphoreType.DMA((2 * NT,)),
                pltpu.SemaphoreType.DMA((2 * NT,)),
                pltpu.SemaphoreType.DMA((6,)),
                pltpu.SemaphoreType.DMA((3 * NT,)),
                pltpu.SemaphoreType.DMA((6,)),
                pltpu.SemaphoreType.DMA((6,)),
                pltpu.SemaphoreType.DMA((NT,)),
                pltpu.SemaphoreType.DMA((NT,)),
            ],
            compiler_params=pltpu.CompilerParams(collective_id=0, has_side_effects=True),
        )(start_states, conduct, velocity)

    in_specs = (P("ta", "gx", "gy"), P("gx", "gy"), P(None, "gx", "gy"))
    return jax.shard_map(
        local, mesh=mesh, in_specs=in_specs, out_specs=P("ta", "gx", "gy"), check_vma=False
    )
```

```python
import functools

import jax
import jax.numpy as jnp
from jax import lax
from jax.experimental import pallas as pl
from jax.experimental.pallas import tpu as pltpu
from jax.sharding import PartitionSpec as P

MESH = pl.DeviceIdType.MESH
NT = 8
TR = 64
TC = 512
LT = 128
HB = 24
WR = TR + 2 * HB
ER = 32
ROWS = [(0, 0, 18), (1, 4, 16), (5, 7, 8)]
FULL = (0, WR)
SPAN = (8, WR - 16)
LAST = (16, WR - 32)
EDGE = {1: (0, 8), 0: (8, 16), -1: (24, 8)}


def roll(value, shift, axis):
    return pltpu.roll(value, shift % value.shape[axis], axis)


def fold(read, base):
    lane = lax.broadcasted_iota(jnp.int32, (8, LT), 1)
    parts = []
    for start, groups in ((40, 3), (0, 4), (32, 4), (0, 3)):
        value = roll(read(start), base, 1)
        for group in range(1, groups):
            moved = roll(read(start + 8 * group), base + 32 * group, 1)
            value = jnp.where(lane < 32 * group, value, moved)
        parts.append(value)
    return parts


def unfold(read, base):
    for start, groups, first in ((0, 3, 0), (8, 4, 3), (16, 4, 7), (24, 3, 11)):
        value = read(start)
        for group in range(groups):
            yield first + group, roll(value, base - 32 * group, 1)


def kernel(
    gxn, gyn, u_ref, cond_ref, vel_ref, out_ref,
    ubuf, wbuf, xbuf, ebuf, xedge, main, other, cwin, cfull, cfold, cedge, coef, state, half, fsend, frecv,
    load_sem, s_main, r_main, s_strip, r_strip, s_edge, r_edge, sc, rc, sf, rf,
):
    ta = lax.axis_index("ta")
    gx = lax.axis_index("gx")
    gy = lax.axis_index("gy")
    even = lax.rem(ta, 2) == 0
    tile_m = ta // 2
    tile_o = lax.rem(tile_m + jnp.where(even, 3, 1), 4)

    def has(dx, dy):
        x, y = gx + dx, gy + dy
        return (x >= 0) & (x < gxn) & (y >= 0) & (y < gyn)

    def ring(step):
        return lax.rem(ta + step, NT)

    barrier = pltpu.get_barrier_semaphore()

    def greet(section, dx, dy):
        pl.semaphore_signal(
            barrier, inc=1, device_id=(section, gx + dx, gy + dy), device_id_type=MESH
        )

    for dx in (-1, 1):

        @pl.when(has(dx, 0))
        def _():
            for step in range(NT):
                greet(ring(step), dx, 0)

    for owner, dy in ((0, -1), (NT - 1, 1)):
        for dx in (-1, 0, 1):

            @pl.when((ta == owner) & has(dx, dy))
            def _():
                for step in range(NT):
                    greet(ring(step), dx, dy)

    for step in range(1, NT):
        greet(ring(step), 0, 0)

    lanes_m = pl.ds(pl.multiple_of(tile_m * LT, LT), LT)
    lanes_o = pl.ds(pl.multiple_of(tile_o * LT, LT), LT)
    loads = [
        pltpu.make_async_copy(u_ref.at[0], ubuf, load_sem.at[0]),
        pltpu.make_async_copy(cond_ref.at[:, lanes_m], main.at[0], load_sem.at[1]),
        pltpu.make_async_copy(cond_ref.at[:, lanes_o], other.at[0], load_sem.at[2]),
        pltpu.make_async_copy(vel_ref.at[:, :, lanes_m], main.at[pl.ds(1, 2)], load_sem.at[3]),
        pltpu.make_async_copy(vel_ref.at[:, :, lanes_o], other.at[pl.ds(1, 2)], load_sem.at[4]),
    ]
    for load in loads:
        load.start()

    count = NT - 1
    for dx in (-1, 1):
        count = count + NT * has(dx, 0).astype(jnp.int32)
    for dy in (-1, 1):
        for dx in (-1, 0, 1):
            count = count + has(dx, dy).astype(jnp.int32)

    xbuf[0, 0:6, :] = jnp.zeros((6, LT), jnp.float32)
    xbuf[0, WR - 6 : WR, :] = jnp.zeros((6, LT), jnp.float32)

    def clear(ref, planes, start, rows):
        ref[:, start : start + rows, :] = jnp.zeros((planes, rows, LT), jnp.float32)

    for dx, start in ((1, 0), (-1, HB + TR)):

        @pl.when(jnp.logical_not(has(-dx, 0)))
        def _():
            clear(xbuf, NT, start, HB)
            clear(cwin, 3, start, HB)

    for owner, dy in ((0, 1), (NT - 1, -1)):
        for dx in (-1, 0, 1):

            @pl.when((ta == owner) & jnp.logical_not(has(-dx, -dy)))
            def _():
                clear(xedge, NT, *EDGE[dx])
                clear(cedge, 3, *EDGE[dx])

    for load in loads:
        load.wait()

    lane = lax.broadcasted_iota(jnp.int32, (TR, LT), 1)
    for owner in range(NT):
        tile = owner // 2
        if owner % 2 == 0:
            mate, keep = (tile + 3) % 4, lane < 96
        else:
            mate, keep = (tile + 1) % 4, lane >= 32
        wbuf[owner] = jnp.where(
            keep, ubuf[:, tile * LT : (tile + 1) * LT], ubuf[:, mate * LT : (mate + 1) * LT]
        )
    for slot, (first, base) in enumerate(((3 * LT, 32), (0, 0))):
        for at, part in enumerate(fold(lambda start: ubuf[start : start + 8, first : first + LT], base)):
            ebuf[slot, 8 * at : 8 * at + 8] = part
    use_m = jnp.where(even, lane, LT - 1 - lane) < 96
    for part in range(3):
        cwin[part, HB : HB + TR, :] = jnp.where(use_m, main[part], other[part])
    for owner, base in ((0, 32), (NT - 1, 0)):

        @pl.when(ta == owner)
        def _():
            for part in range(3):
                for at, value in enumerate(fold(lambda start: other[part, start : start + 8], base)):
                    cfold[part, 8 * at : 8 * at + 8] = value

    xbuf[ta, HB : HB + TR] = wbuf[ta]
    pl.semaphore_wait(barrier, count)

    def main_copy(owner, section):
        return pltpu.make_async_remote_copy(
            src_ref=wbuf.at[owner],
            dst_ref=xbuf.at[section, pl.ds(HB, TR)],
            send_sem=s_main.at[owner],
            recv_sem=r_main.at[section],
            device_id=(owner, gx, gy),
            device_id_type=MESH,
        )

    def strip_copy(owner, section, dx, rows, here=False):
        if dx < 0:
            src, dst = pl.ds(0, rows), pl.ds(HB + TR, rows)
        else:
            src, dst = pl.ds(TR - rows, rows), pl.ds(HB - rows, rows)
        side = (dx + 1) // 2
        return pltpu.make_async_remote_copy(
            src_ref=wbuf.at[owner, src],
            dst_ref=xbuf.at[section, dst],
            send_sem=s_strip.at[NT * side + owner],
            recv_sem=r_strip.at[NT * side + section],
            device_id=(ta, gx, gy) if here else (owner, gx + dx, gy),
            device_id_type=MESH,
        )

    def edge_copy(section, dx, dy, here=False):
        slot, owner = (0, 0) if dy > 0 else (1, NT - 1)
        start, rows = EDGE[dx]
        return pltpu.make_async_remote_copy(
            src_ref=ebuf.at[slot, pl.ds(start, rows)],
            dst_ref=xedge.at[section, pl.ds(start, rows)],
            send_sem=s_edge.at[3 * slot + dx + 1],
            recv_sem=r_edge.at[3 * section + dx + 1],
            device_id=(ta, gx, gy) if here else (ring(lax.rem(owner + NT - ta, NT)), gx + dx, gy + dy),
            device_id_type=MESH,
        )

    def coef_copy(dx, dy, here=False):
        if dy == 0:
            if dx < 0:
                src, dst = pl.ds(HB, HB), pl.ds(HB + TR, HB)
            else:
                src, dst = pl.ds(TR, HB), pl.ds(0, HB)
            src, dst = cwin.at[:, src, :], cwin.at[:, dst, :]
        else:
            place = pl.ds(*EDGE[dx])
            src, dst = cfold.at[:, place, :], cedge.at[:, place, :]
        at = 3 * (1 if dy else 0) + dx + 1
        return pltpu.make_async_remote_copy(
            src_ref=src,
            dst_ref=dst,
            send_sem=sc.at[at],
            recv_sem=rc.at[at],
            device_id=(ta, gx, gy) if here else (ta, gx + dx, gy + dy),
            device_id_type=MESH,
        )

    coef_dirs = [(-1, 0, None), (1, 0, None)]
    coef_dirs += [(dx, 1, 0) for dx in (-1, 0, 1)] + [(dx, -1, NT - 1) for dx in (-1, 0, 1)]

    def sends(act):
        for dx in (-1, 1, 0):
            for dy in (-1, 1):

                @pl.when(has(dx, dy))
                def _():
                    act(edge_copy(ta, dx, dy))

        for dx, dy, only in coef_dirs:
            near = has(dx, dy)

            @pl.when(near if only is None else near & (ta == only))
            def _():
                act(coef_copy(dx, dy))

        for first, last, rows in ROWS:

            @pl.when((ta >= first) & (ta <= last))
            def _():
                for dx in (-1, 1):

                    @pl.when(has(dx, 0))
                    def _():
                        for step in range(NT):
                            act(strip_copy(ring(step), ta, dx, rows))

        for step in range(1, NT):
            act(main_copy(ring(step), ta))

    sends(lambda copy: copy.start())

    for dx, dy, only in coef_dirs:
        near = has(-dx, -dy)

        @pl.when(near if only is None else near & (ta == only))
        def _():
            coef_copy(dx, dy, True).wait_recv()

    cfull[...] = cwin[...]
    edge_lane = lax.broadcasted_iota(jnp.int32, (8, LT), 1)
    for owner, base in ((0, 96), (NT - 1, 0)):

        @pl.when(ta == owner)
        def _():
            mine = (edge_lane >= base) & (edge_lane < base + 32)
            for part in range(3):
                for at, value in unfold(lambda start: cedge[part, start : start + 8], base):
                    rows = slice(8 * at, 8 * at + 8)
                    cfull[part, rows] = jnp.where(mine, value, cfull[part, rows])

    wlane = lax.broadcasted_iota(jnp.int32, (WR, LT), 1)
    row = lax.broadcasted_iota(jnp.int32, (WR, LT), 0)

    def mean(part):
        value = cfull[part]
        value = value + roll(value, -1, 1)
        return value + roll(value, -1, 0)

    stiff = mean(0) * (0.25 * 0.1 / 6.0)
    vx = mean(1) * (0.25 * 0.1 / 8.0)
    vy = mean(2) * (0.25 * 0.1 / 8.0)
    gam = vx + vy
    kap = vx - vy
    column = (
        gy * TC + ta * 64 + jnp.where(
            even,
            jnp.where(wlane < 96, wlane, wlane - LT),
            jnp.where(wlane < 32, wlane + 64, wlane - 64),
        )
    )
    line = gx * TR + row - HB
    inside = (column >= 0) & (column < gyn * TC) & (line >= 0) & (line < gxn * TR)

    def put(slot, shift, value):
        coef[slot] = roll(jnp.where(inside, value, 0.0), shift, 0)

    def before(value):
        return roll(value, 1, 0)

    def left(value):
        return roll(value, 1, 1)

    put(0, 0, (4.0 * stiff - gam) + before(4.0 * stiff + kap) + left(4.0 * stiff - kap + before(4.0 * stiff + gam)))
    put(1, 0, (-stiff - kap) + before(gam - stiff))
    put(2, 0, left((-stiff - gam) + before(kap - stiff)))
    put(3, 1, (kap - stiff) + left(gam - stiff))
    put(4, 1, gam - 2.0 * stiff)
    put(5, 1, left(kap - 2.0 * stiff))
    put(6, -1, before((-stiff - gam) + left(-stiff - kap)))
    put(7, -1, before(-kap - 2.0 * stiff))
    put(8, -1, left(before(-gam - 2.0 * stiff)))

    def rate(value, span):
        start, rows = span
        high = roll(value, -1, 1)
        low = roll(value, 1, 1)

        def line_sum(slot):
            return (
                coef[slot, start : start + rows] * value
                + coef[slot + 1, start : start + rows] * high
                + coef[slot + 2, start : start + rows] * low
            )

        return line_sum(0) + roll(line_sum(3), -1, 0) + roll(line_sum(6), 1, 0)

    def trim(value, old, new):
        skip = new[0] - old[0]
        return value[skip : skip + new[1]]

    def result_copy(section):
        return pltpu.make_async_remote_copy(
            src_ref=fsend.at[section],
            dst_ref=frecv.at[ta],
            send_sem=sf.at[section],
            recv_sem=rf.at[ta],
            device_id=(section, gx, gy),
            device_id_type=MESH,
        )

    flane = lax.broadcasted_iota(jnp.int32, (TR // 2, LT), 1)
    fmain = jnp.where(even, flane, LT - 1 - flane) < 64
    def arrive(section, halo, span):
        @pl.when(ta != section)
        def _():
            main_copy(section, section).wait_recv()

        for dx in (-1, 1):

            @pl.when(has(-dx, 0))
            def _():
                strip_copy(section, section, dx, halo, True).wait_recv()

        for owner, dy, base in ((0, 1, 96), (NT - 1, -1, 0)):

            @pl.when(ta == owner)
            def _():
                for dx in (-1, 0, 1):

                    @pl.when(has(-dx, -dy))
                    def _():
                        edge_copy(section, dx, dy, True).wait_recv()

                mine = (edge_lane >= base) & (edge_lane < base + 32)
                for at, value in unfold(lambda start: xedge[section, start : start + 8], base):
                    if span[0] <= 8 * at < span[0] + span[1]:
                        place = slice(8 * at, 8 * at + 8)
                        xbuf[section, place] = jnp.where(mine, value, xbuf[section, place])

        value = xbuf[section, span[0] : span[0] + span[1]]
        return 0.5 * rate(value - 0.25 * rate(value, span), span)

    def advance(value, half, span):
        return value - 2.0 * rate(value - rate(value - half, span), span)

    def give(section, value, span):
        tile = trim(value, span, (HB, TR))
        fsend[section] = jnp.where(fmain, tile[: TR // 2], roll(tile[TR // 2 :], 64, 1))

        @pl.when(ta != section)
        def _():
            result_copy(section).start()

    inner = slice(SPAN[0], SPAN[0] + SPAN[1])
    last = slice(LAST[0], LAST[0] + LAST[1])
    half[...] = arrive(0, 18, FULL)
    state[inner] = xbuf[0, inner]

    def step(section, carry, halo, span):
        rows = slice(span[0], span[0] + span[1])
        after = arrive(section, halo, span)
        value = advance(state[rows], half[rows], span)
        state[rows] = value
        half[rows] = after
        give(section - 1, value, span)
        return carry

    lax.fori_loop(1, 5, functools.partial(step, halo=16, span=SPAN), 0)
    lax.fori_loop(5, NT, functools.partial(step, halo=8, span=LAST), 0)
    give(NT - 1, advance(state[last], half[last], LAST), LAST)

    frecv[ta] = fsend[ta]

    for step in range(1, NT):
        peer = lax.rem(ta + step, NT)
        pltpu.make_async_remote_copy(
            src_ref=fsend.at[peer],
            dst_ref=frecv.at[peer],
            send_sem=sf.at[peer],
            recv_sem=rf.at[peer],
            device_id=(peer, gx, gy),
            device_id_type=MESH,
        ).wait_recv()

    for tile in range(4):
        lower, upper = frecv[2 * tile], frecv[2 * tile + 1]
        lanes = slice(tile * LT, (tile + 1) * LT)
        out_ref[0, : TR // 2, lanes] = jnp.where(flane < 64, lower, upper)
        out_ref[0, TR // 2 :, lanes] = roll(jnp.where(flane < 64, upper, lower), 64, 1)

    sends(lambda copy: copy.wait_send())
    for step in range(1, NT):
        result_copy(lax.rem(ta + step, NT)).wait_send()


def solution(mesh):
    gxn, gyn = mesh.shape["gx"], mesh.shape["gy"]

    def local(start_states, conduct, velocity):
        return pl.pallas_call(
            functools.partial(kernel, gxn, gyn),
            out_shape=pltpu.VMEM((1, TR, TC), jnp.float32),
            in_specs=[pl.BlockSpec(memory_space=pl.ANY)] * 3,
            out_specs=pl.BlockSpec(memory_space=pltpu.VMEM),
            scratch_shapes=[
                pltpu.VMEM((TR, TC), jnp.float32),
                pltpu.VMEM((NT, TR, LT), jnp.float32),
                pltpu.VMEM((NT, WR, LT), jnp.float32),
                pltpu.VMEM((2, ER, LT), jnp.float32),
                pltpu.VMEM((NT, ER, LT), jnp.float32),
                pltpu.VMEM((3, TR, LT), jnp.float32),
                pltpu.VMEM((3, TR, LT), jnp.float32),
                pltpu.VMEM((3, WR, LT), jnp.float32),
                pltpu.VMEM((3, WR, LT), jnp.float32),
                pltpu.VMEM((3, ER, LT), jnp.float32),
                pltpu.VMEM((3, ER, LT), jnp.float32),
                pltpu.VMEM((9, WR, LT), jnp.float32),
                pltpu.VMEM((WR, LT), jnp.float32),
                pltpu.VMEM((WR, LT), jnp.float32),
                pltpu.VMEM((NT, TR // 2, LT), jnp.float32),
                pltpu.VMEM((NT, TR // 2, LT), jnp.float32),
                pltpu.SemaphoreType.DMA((5,)),
                pltpu.SemaphoreType.DMA((NT,)),
                pltpu.SemaphoreType.DMA((NT,)),
                pltpu.SemaphoreType.DMA((2 * NT,)),
                pltpu.SemaphoreType.DMA((2 * NT,)),
                pltpu.SemaphoreType.DMA((6,)),
                pltpu.SemaphoreType.DMA((3 * NT,)),
                pltpu.SemaphoreType.DMA((6,)),
                pltpu.SemaphoreType.DMA((6,)),
                pltpu.SemaphoreType.DMA((NT,)),
                pltpu.SemaphoreType.DMA((NT,)),
            ],
            compiler_params=pltpu.CompilerParams(collective_id=0, has_side_effects=True),
        )(start_states, conduct, velocity)

    in_specs = (P("ta", "gx", "gy"), P("gx", "gy"), P(None, "gx", "gy"))
    return jax.shard_map(
        local, mesh=mesh, in_specs=in_specs, out_specs=P("ta", "gx", "gy"), check_vma=False
    )
```

```python
import functools

import jax
import jax.numpy as jnp
from jax import lax
from jax.experimental import pallas as pl
from jax.experimental.pallas import tpu as pltpu
from jax.sharding import PartitionSpec as P

MESH = pl.DeviceIdType.MESH
NT = 8
TR = 64
TC = 512
LT = 128
HB = 24
RAD = 18
ORDER = (4, 3, 5, 2, 6, 1, 7, 0)
WR = TR + 2 * HB
ER = 32
ROWS = [(0, 0, RAD), (1, 4, 16), (5, 7, 8)]
FULL = (0, WR)
SPAN = (8, WR - 16)
LAST = (16, WR - 32)
EDGE = {1: (0, 8), 0: (8, 16), -1: (24, 8)}


def roll(value, shift, axis):
    return pltpu.roll(value, shift % value.shape[axis], axis)


def fold(read, base):
    lane = lax.broadcasted_iota(jnp.int32, (8, LT), 1)
    parts = []
    for start, groups in ((40, 3), (0, 4), (32, 4), (0, 3)):
        value = roll(read(start), base, 1)
        for group in range(1, groups):
            moved = roll(read(start + 8 * group), base + 32 * group, 1)
            value = jnp.where(lane < 32 * group, value, moved)
        parts.append(value)
    return parts


def unfold(read, base):
    for start, groups, first in ((0, 3, 0), (8, 4, 3), (16, 4, 7), (24, 3, 11)):
        value = read(start)
        for group in range(groups):
            yield first + group, roll(value, base - 32 * group, 1)


def kernel(
    gxn, gyn, u_ref, cond_ref, vel_ref, out_ref,
    ubuf, wbuf, xbuf, ebuf, xedge, main, other, cwin, cfull, cfold, cedge, coef, state, half, fsend, frecv,
    load_sem, s_main, r_main, s_strip, r_strip, s_edge, r_edge, sc, rc, sf, rf,
):
    ta = lax.axis_index("ta")
    gx = lax.axis_index("gx")
    gy = lax.axis_index("gy")
    even = lax.rem(ta, 2) == 0
    tile_m = ta // 2
    tile_o = lax.rem(tile_m + jnp.where(even, 3, 1), 4)

    def has(dx, dy):
        x, y = gx + dx, gy + dy
        return (x >= 0) & (x < gxn) & (y >= 0) & (y < gyn)

    def ring(step):
        return lax.rem(ta + step, NT)

    barrier = pltpu.get_barrier_semaphore()

    def greet(section, dx, dy):
        pl.semaphore_signal(
            barrier, inc=1, device_id=(section, gx + dx, gy + dy), device_id_type=MESH
        )

    for dx in (-1, 1):

        @pl.when(has(dx, 0))
        def _():
            for step in range(NT):
                greet(ring(step), dx, 0)

    for owner, dy in ((0, -1), (NT - 1, 1)):
        for dx in (-1, 0, 1):

            @pl.when((ta == owner) & has(dx, dy))
            def _():
                for step in range(NT):
                    greet(ring(step), dx, dy)

    for step in range(1, NT):
        greet(ring(step), 0, 0)

    lanes_m = pl.ds(pl.multiple_of(tile_m * LT, LT), LT)
    lanes_o = pl.ds(pl.multiple_of(tile_o * LT, LT), LT)
    loads = [
        pltpu.make_async_copy(u_ref.at[0], ubuf, load_sem.at[0]),
        pltpu.make_async_copy(cond_ref.at[:, lanes_m], main.at[0], load_sem.at[1]),
        pltpu.make_async_copy(cond_ref.at[:, lanes_o], other.at[0], load_sem.at[2]),
        pltpu.make_async_copy(vel_ref.at[:, :, lanes_m], main.at[pl.ds(1, 2)], load_sem.at[3]),
        pltpu.make_async_copy(vel_ref.at[:, :, lanes_o], other.at[pl.ds(1, 2)], load_sem.at[4]),
    ]
    for load in loads:
        load.start()

    count = NT - 1
    for dx in (-1, 1):
        count = count + NT * has(dx, 0).astype(jnp.int32)
    for dy in (-1, 1):
        for dx in (-1, 0, 1):
            count = count + has(dx, dy).astype(jnp.int32)

    xbuf[0, 0:6, :] = jnp.zeros((6, LT), jnp.float32)
    xbuf[0, WR - 6 : WR, :] = jnp.zeros((6, LT), jnp.float32)
    cwin[:, 0:6, :] = jnp.zeros((3, 6, LT), jnp.float32)
    cwin[:, WR - 6 : WR, :] = jnp.zeros((3, 6, LT), jnp.float32)

    def clear(ref, planes, start, rows):
        ref[:, start : start + rows, :] = jnp.zeros((planes, rows, LT), jnp.float32)

    for dx, start in ((1, 0), (-1, HB + TR)):

        @pl.when(jnp.logical_not(has(-dx, 0)))
        def _():
            clear(xbuf, NT, start, HB)
            clear(cwin, 3, start, HB)

    for owner, dy in ((0, 1), (NT - 1, -1)):
        for dx in (-1, 0, 1):

            @pl.when((ta == owner) & jnp.logical_not(has(-dx, -dy)))
            def _():
                clear(xedge, NT, *EDGE[dx])
                clear(cedge, 3, *EDGE[dx])

    for load in loads:
        load.wait()

    lane = lax.broadcasted_iota(jnp.int32, (TR, LT), 1)
    for owner in range(NT):
        tile = owner // 2
        if owner % 2 == 0:
            mate, keep = (tile + 3) % 4, lane < 96
        else:
            mate, keep = (tile + 1) % 4, lane >= 32
        wbuf[owner] = jnp.where(
            keep, ubuf[:, tile * LT : (tile + 1) * LT], ubuf[:, mate * LT : (mate + 1) * LT]
        )
    for slot, (first, base) in enumerate(((3 * LT, 32), (0, 0))):
        for at, part in enumerate(fold(lambda start: ubuf[start : start + 8, first : first + LT], base)):
            ebuf[slot, 8 * at : 8 * at + 8] = part
    use_m = jnp.where(even, lane, LT - 1 - lane) < 96
    for part in range(3):
        cwin[part, HB : HB + TR, :] = jnp.where(use_m, main[part], other[part])
    for owner, base in ((0, 32), (NT - 1, 0)):

        @pl.when(ta == owner)
        def _():
            for part in range(3):
                for at, value in enumerate(fold(lambda start: other[part, start : start + 8], base)):
                    cfold[part, 8 * at : 8 * at + 8] = value

    xbuf[ta, HB : HB + TR] = wbuf[ta]
    pl.semaphore_wait(barrier, count)

    def main_copy(owner, section):
        return pltpu.make_async_remote_copy(
            src_ref=wbuf.at[owner],
            dst_ref=xbuf.at[section, pl.ds(HB, TR)],
            send_sem=s_main.at[owner],
            recv_sem=r_main.at[section],
            device_id=(owner, gx, gy),
            device_id_type=MESH,
        )

    def strip_copy(owner, section, dx, rows, here=False):
        if dx < 0:
            src, dst = pl.ds(0, rows), pl.ds(HB + TR, rows)
        else:
            src, dst = pl.ds(TR - rows, rows), pl.ds(HB - rows, rows)
        side = (dx + 1) // 2
        return pltpu.make_async_remote_copy(
            src_ref=wbuf.at[owner, src],
            dst_ref=xbuf.at[section, dst],
            send_sem=s_strip.at[NT * side + owner],
            recv_sem=r_strip.at[NT * side + section],
            device_id=(ta, gx, gy) if here else (owner, gx + dx, gy),
            device_id_type=MESH,
        )

    def edge_copy(section, dx, dy, here=False):
        slot, owner = (0, 0) if dy > 0 else (1, NT - 1)
        start, rows = EDGE[dx]
        return pltpu.make_async_remote_copy(
            src_ref=ebuf.at[slot, pl.ds(start, rows)],
            dst_ref=xedge.at[section, pl.ds(start, rows)],
            send_sem=s_edge.at[3 * slot + dx + 1],
            recv_sem=r_edge.at[3 * section + dx + 1],
            device_id=(ta, gx, gy) if here else (ring(lax.rem(owner + NT - ta, NT)), gx + dx, gy + dy),
            device_id_type=MESH,
        )

    def coef_copy(dx, dy, here=False):
        if dy == 0:
            if dx < 0:
                src, dst = pl.ds(HB, RAD), pl.ds(HB + TR, RAD)
            else:
                src, dst = pl.ds(HB + TR - RAD, RAD), pl.ds(HB - RAD, RAD)
            src, dst = cwin.at[:, src, :], cwin.at[:, dst, :]
        else:
            place = pl.ds(*EDGE[dx])
            src, dst = cfold.at[:, place, :], cedge.at[:, place, :]
        at = 3 * (1 if dy else 0) + dx + 1
        return pltpu.make_async_remote_copy(
            src_ref=src,
            dst_ref=dst,
            send_sem=sc.at[at],
            recv_sem=rc.at[at],
            device_id=(ta, gx, gy) if here else (ta, gx + dx, gy + dy),
            device_id_type=MESH,
        )

    coef_dirs = [(-1, 0, None), (1, 0, None)]
    coef_dirs += [(dx, 1, 0) for dx in (-1, 0, 1)] + [(dx, -1, NT - 1) for dx in (-1, 0, 1)]

    def sends(act):
        for dx in (-1, 1, 0):
            for dy in (-1, 1):

                @pl.when(has(dx, dy))
                def _():
                    act(edge_copy(ta, dx, dy))

        for dx, dy, only in coef_dirs:
            near = has(dx, dy)

            @pl.when(near if only is None else near & (ta == only))
            def _():
                act(coef_copy(dx, dy))

        for first, last, rows in ROWS:

            @pl.when((ta >= first) & (ta <= last))
            def _():
                for step in ORDER:
                    for dx in (-1, 1):

                        @pl.when(has(dx, 0))
                        def _():
                            act(strip_copy(ring(step), ta, dx, rows))

        for step in ORDER[:-1]:
            act(main_copy(ring(step), ta))

    sends(lambda copy: copy.start())

    for dx, dy, only in coef_dirs:
        near = has(-dx, -dy)

        @pl.when(near if only is None else near & (ta == only))
        def _():
            coef_copy(dx, dy, True).wait_recv()

    cfull[...] = cwin[...]
    edge_lane = lax.broadcasted_iota(jnp.int32, (8, LT), 1)
    for owner, base in ((0, 96), (NT - 1, 0)):

        @pl.when(ta == owner)
        def _():
            mine = (edge_lane >= base) & (edge_lane < base + 32)
            for part in range(3):
                for at, value in unfold(lambda start: cedge[part, start : start + 8], base):
                    rows = slice(8 * at, 8 * at + 8)
                    cfull[part, rows] = jnp.where(mine, value, cfull[part, rows])

    wlane = lax.broadcasted_iota(jnp.int32, (WR, LT), 1)
    row = lax.broadcasted_iota(jnp.int32, (WR, LT), 0)

    def mean(part):
        value = cfull[part]
        value = value + roll(value, -1, 1)
        return value + roll(value, -1, 0)

    stiff = mean(0) * (0.25 * 0.1 / 6.0)
    vx = mean(1) * (0.25 * 0.1 / 8.0)
    vy = mean(2) * (0.25 * 0.1 / 8.0)
    gam = vx + vy
    kap = vx - vy
    column = (
        gy * TC + ta * 64 + jnp.where(
            even,
            jnp.where(wlane < 96, wlane, wlane - LT),
            jnp.where(wlane < 32, wlane + 64, wlane - 64),
        )
    )
    line = gx * TR + row - HB
    inside = (column >= 0) & (column < gyn * TC) & (line >= 0) & (line < gxn * TR)

    def put(slot, shift, value):
        coef[slot] = roll(jnp.where(inside, value, 0.0), shift, 0)

    def before(value):
        return roll(value, 1, 0)

    def left(value):
        return roll(value, 1, 1)

    put(0, 0, (4.0 * stiff - gam) + before(4.0 * stiff + kap) + left(4.0 * stiff - kap + before(4.0 * stiff + gam)))
    put(1, 0, (-stiff - kap) + before(gam - stiff))
    put(2, 0, left((-stiff - gam) + before(kap - stiff)))
    put(3, 1, (kap - stiff) + left(gam - stiff))
    put(4, 1, gam - 2.0 * stiff)
    put(5, 1, left(kap - 2.0 * stiff))
    put(6, -1, before((-stiff - gam) + left(-stiff - kap)))
    put(7, -1, before(-kap - 2.0 * stiff))
    put(8, -1, left(before(-gam - 2.0 * stiff)))

    def rate(value, span):
        start, rows = span
        high = roll(value, -1, 1)
        low = roll(value, 1, 1)

        def line_sum(slot):
            return (
                coef[slot, start : start + rows] * value
                + coef[slot + 1, start : start + rows] * high
                + coef[slot + 2, start : start + rows] * low
            )

        return line_sum(0) + roll(line_sum(3), -1, 0) + roll(line_sum(6), 1, 0)

    def trim(value, old, new):
        skip = new[0] - old[0]
        return value[skip : skip + new[1]]

    def result_copy(section):
        return pltpu.make_async_remote_copy(
            src_ref=fsend.at[section],
            dst_ref=frecv.at[ta],
            send_sem=sf.at[section],
            recv_sem=rf.at[ta],
            device_id=(section, gx, gy),
            device_id_type=MESH,
        )

    flane = lax.broadcasted_iota(jnp.int32, (TR // 2, LT), 1)
    fmain = jnp.where(even, flane, LT - 1 - flane) < 64
    def arrive(section, halo, span):
        @pl.when(ta != section)
        def _():
            main_copy(section, section).wait_recv()

        for dx in (-1, 1):

            @pl.when(has(-dx, 0))
            def _():
                strip_copy(section, section, dx, halo, True).wait_recv()

        for owner, dy, base in ((0, 1, 96), (NT - 1, -1, 0)):

            @pl.when(ta == owner)
            def _():
                for dx in (-1, 0, 1):

                    @pl.when(has(-dx, -dy))
                    def _():
                        edge_copy(section, dx, dy, True).wait_recv()

                mine = (edge_lane >= base) & (edge_lane < base + 32)
                for at, value in unfold(lambda start: xedge[section, start : start + 8], base):
                    if span[0] <= 8 * at < span[0] + span[1]:
                        place = slice(8 * at, 8 * at + 8)
                        xbuf[section, place] = jnp.where(mine, value, xbuf[section, place])

        value = xbuf[section, span[0] : span[0] + span[1]]
        return 0.5 * rate(value - 0.25 * rate(value, span), span)

    def advance(value, half, span):
        return value - 2.0 * rate(value - rate(value - half, span), span)

    def give(section, value, span):
        tile = trim(value, span, (HB, TR))
        fsend[section] = jnp.where(fmain, tile[: TR // 2], roll(tile[TR // 2 :], 64, 1))

        @pl.when(ta != section)
        def _():
            result_copy(section).start()

    inner = slice(SPAN[0], SPAN[0] + SPAN[1])
    last = slice(LAST[0], LAST[0] + LAST[1])
    half[...] = arrive(0, RAD, FULL)
    state[inner] = xbuf[0, inner]

    def step(section, carry, halo, span):
        rows = slice(span[0], span[0] + span[1])
        after = arrive(section, halo, span)
        value = advance(state[rows], half[rows], span)
        state[rows] = value
        half[rows] = after
        give(section - 1, value, span)
        return carry

    lax.fori_loop(1, 5, functools.partial(step, halo=16, span=SPAN), 0)
    lax.fori_loop(5, NT, functools.partial(step, halo=8, span=LAST), 0)
    give(NT - 1, advance(state[last], half[last], LAST), LAST)

    frecv[ta] = fsend[ta]

    sends(lambda copy: copy.wait_send())
    for step in range(1, NT):
        result_copy(lax.rem(ta + step, NT)).wait_send()

    for step in range(1, NT):
        peer = lax.rem(ta + step, NT)
        pltpu.make_async_remote_copy(
            src_ref=fsend.at[peer],
            dst_ref=frecv.at[peer],
            send_sem=sf.at[peer],
            recv_sem=rf.at[peer],
            device_id=(peer, gx, gy),
            device_id_type=MESH,
        ).wait_recv()

    for tile in range(4):
        lower, upper = frecv[2 * tile], frecv[2 * tile + 1]
        lanes = slice(tile * LT, (tile + 1) * LT)
        out_ref[0, : TR // 2, lanes] = jnp.where(flane < 64, lower, upper)
        out_ref[0, TR // 2 :, lanes] = roll(jnp.where(flane < 64, upper, lower), 64, 1)


def solution(mesh):
    gxn, gyn = mesh.shape["gx"], mesh.shape["gy"]

    def local(start_states, conduct, velocity):
        return pl.pallas_call(
            functools.partial(kernel, gxn, gyn),
            out_shape=pltpu.VMEM((1, TR, TC), jnp.float32),
            in_specs=[pl.BlockSpec(memory_space=pl.ANY)] * 3,
            out_specs=pl.BlockSpec(memory_space=pltpu.VMEM),
            scratch_shapes=[
                pltpu.VMEM((TR, TC), jnp.float32),
                pltpu.VMEM((NT, TR, LT), jnp.float32),
                pltpu.VMEM((NT, WR, LT), jnp.float32),
                pltpu.VMEM((2, ER, LT), jnp.float32),
                pltpu.VMEM((NT, ER, LT), jnp.float32),
                pltpu.VMEM((3, TR, LT), jnp.float32),
                pltpu.VMEM((3, TR, LT), jnp.float32),
                pltpu.VMEM((3, WR, LT), jnp.float32),
                pltpu.VMEM((3, WR, LT), jnp.float32),
                pltpu.VMEM((3, ER, LT), jnp.float32),
                pltpu.VMEM((3, ER, LT), jnp.float32),
                pltpu.VMEM((9, WR, LT), jnp.float32),
                pltpu.VMEM((WR, LT), jnp.float32),
                pltpu.VMEM((WR, LT), jnp.float32),
                pltpu.VMEM((NT, TR // 2, LT), jnp.float32),
                pltpu.VMEM((NT, TR // 2, LT), jnp.float32),
                pltpu.SemaphoreType.DMA((5,)),
                pltpu.SemaphoreType.DMA((NT,)),
                pltpu.SemaphoreType.DMA((NT,)),
                pltpu.SemaphoreType.DMA((2 * NT,)),
                pltpu.SemaphoreType.DMA((2 * NT,)),
                pltpu.SemaphoreType.DMA((6,)),
                pltpu.SemaphoreType.DMA((3 * NT,)),
                pltpu.SemaphoreType.DMA((6,)),
                pltpu.SemaphoreType.DMA((6,)),
                pltpu.SemaphoreType.DMA((NT,)),
                pltpu.SemaphoreType.DMA((NT,)),
            ],
            compiler_params=pltpu.CompilerParams(collective_id=0, has_side_effects=True),
        )(start_states, conduct, velocity)

    in_specs = (P("ta", "gx", "gy"), P("gx", "gy"), P(None, "gx", "gy"))
    return jax.shard_map(
        local, mesh=mesh, in_specs=in_specs, out_specs=P("ta", "gx", "gy"), check_vma=False
    )
```

```python
import functools

import jax
import jax.numpy as jnp
from jax import lax
from jax.experimental import pallas as pl
from jax.experimental.pallas import tpu as pltpu
from jax.sharding import PartitionSpec as P

MESH = pl.DeviceIdType.MESH
NT = 8
TR = 64
TC = 512
LT = 128
HB = 24
RAD = 18
ORDER = (5, 4, 3, 7, 2, 6, 1, 0)
WR = TR + 2 * HB
ER = 32
ROWS = [(0, 0, RAD), (1, 4, 16), (5, 7, 8)]
FULL = (0, WR)
SPAN = (8, WR - 16)
LAST = (16, WR - 32)
EDGE = {1: (0, 8), 0: (8, 16), -1: (24, 8)}


def roll(value, shift, axis):
    return pltpu.roll(value, shift % value.shape[axis], axis)


def fold(read, base):
    lane = lax.broadcasted_iota(jnp.int32, (8, LT), 1)
    parts = []
    for start, groups in ((40, 3), (0, 4), (32, 4), (0, 3)):
        value = roll(read(start), base, 1)
        for group in range(1, groups):
            moved = roll(read(start + 8 * group), base + 32 * group, 1)
            value = jnp.where(lane < 32 * group, value, moved)
        parts.append(value)
    return parts


def unfold(read, base):
    for start, groups, first in ((0, 3, 0), (8, 4, 3), (16, 4, 7), (24, 3, 11)):
        value = read(start)
        for group in range(groups):
            yield first + group, roll(value, base - 32 * group, 1)


def kernel(
    gxn, gyn, u_ref, cond_ref, vel_ref, out_ref,
    ubuf, wbuf, xbuf, ebuf, xedge, main, other, cwin, cfull, cfold, cedge, coef, state, half, fsend, frecv,
    load_sem, s_main, r_main, s_strip, r_strip, s_edge, r_edge, sc, rc, sf, rf,
):
    ta = lax.axis_index("ta")
    gx = lax.axis_index("gx")
    gy = lax.axis_index("gy")
    even = lax.rem(ta, 2) == 0
    tile_m = ta // 2
    tile_o = lax.rem(tile_m + jnp.where(even, 3, 1), 4)

    def has(dx, dy):
        x, y = gx + dx, gy + dy
        return (x >= 0) & (x < gxn) & (y >= 0) & (y < gyn)

    def ring(step):
        return lax.rem(ta + step, NT)

    def mirror(step):
        return ring(jnp.where(even, step, NT - step))

    barrier = pltpu.get_barrier_semaphore()

    def greet(section, dx, dy):
        pl.semaphore_signal(
            barrier, inc=1, device_id=(section, gx + dx, gy + dy), device_id_type=MESH
        )

    for dx in (-1, 1):

        @pl.when(has(dx, 0))
        def _():
            for step in range(NT):
                greet(ring(step), dx, 0)

    for owner, dy in ((0, -1), (NT - 1, 1)):
        for dx in (-1, 0, 1):

            @pl.when((ta == owner) & has(dx, dy))
            def _():
                for step in range(NT):
                    greet(ring(step), dx, dy)

    for step in range(1, NT):
        greet(ring(step), 0, 0)

    lanes_m = pl.ds(pl.multiple_of(tile_m * LT, LT), LT)
    lanes_o = pl.ds(pl.multiple_of(tile_o * LT, LT), LT)
    loads = [
        pltpu.make_async_copy(u_ref.at[0], ubuf, load_sem.at[0]),
        pltpu.make_async_copy(cond_ref.at[:, lanes_m], main.at[0], load_sem.at[1]),
        pltpu.make_async_copy(cond_ref.at[:, lanes_o], other.at[0], load_sem.at[2]),
        pltpu.make_async_copy(vel_ref.at[:, :, lanes_m], main.at[pl.ds(1, 2)], load_sem.at[3]),
        pltpu.make_async_copy(vel_ref.at[:, :, lanes_o], other.at[pl.ds(1, 2)], load_sem.at[4]),
    ]
    for load in loads:
        load.start()

    count = NT - 1
    for dx in (-1, 1):
        count = count + NT * has(dx, 0).astype(jnp.int32)
    for dy in (-1, 1):
        for dx in (-1, 0, 1):
            count = count + has(dx, dy).astype(jnp.int32)

    xbuf[0, 0:6, :] = jnp.zeros((6, LT), jnp.float32)
    xbuf[0, WR - 6 : WR, :] = jnp.zeros((6, LT), jnp.float32)
    cwin[:, 0:6, :] = jnp.zeros((3, 6, LT), jnp.float32)
    cwin[:, WR - 6 : WR, :] = jnp.zeros((3, 6, LT), jnp.float32)

    def clear(ref, planes, start, rows):
        ref[:, start : start + rows, :] = jnp.zeros((planes, rows, LT), jnp.float32)

    for dx, start in ((1, 0), (-1, HB + TR)):

        @pl.when(jnp.logical_not(has(-dx, 0)))
        def _():
            clear(xbuf, NT, start, HB)
            clear(cwin, 3, start, HB)

    for owner, dy in ((0, 1), (NT - 1, -1)):
        for dx in (-1, 0, 1):

            @pl.when((ta == owner) & jnp.logical_not(has(-dx, -dy)))
            def _():
                clear(xedge, NT, *EDGE[dx])
                clear(cedge, 3, *EDGE[dx])

    for load in loads:
        load.wait()

    lane = lax.broadcasted_iota(jnp.int32, (TR, LT), 1)
    for owner in range(NT):
        tile = owner // 2
        if owner % 2 == 0:
            mate, keep = (tile + 3) % 4, lane < 96
        else:
            mate, keep = (tile + 1) % 4, lane >= 32
        wbuf[owner] = jnp.where(
            keep, ubuf[:, tile * LT : (tile + 1) * LT], ubuf[:, mate * LT : (mate + 1) * LT]
        )
    for slot, (first, base) in enumerate(((3 * LT, 32), (0, 0))):
        for at, part in enumerate(fold(lambda start: ubuf[start : start + 8, first : first + LT], base)):
            ebuf[slot, 8 * at : 8 * at + 8] = part
    use_m = jnp.where(even, lane, LT - 1 - lane) < 96
    for part in range(3):
        cwin[part, HB : HB + TR, :] = jnp.where(use_m, main[part], other[part])
    for owner, base in ((0, 32), (NT - 1, 0)):

        @pl.when(ta == owner)
        def _():
            for part in range(3):
                for at, value in enumerate(fold(lambda start: other[part, start : start + 8], base)):
                    cfold[part, 8 * at : 8 * at + 8] = value

    xbuf[ta, HB : HB + TR] = wbuf[ta]
    pl.semaphore_wait(barrier, count)

    def main_copy(owner, section):
        return pltpu.make_async_remote_copy(
            src_ref=wbuf.at[owner],
            dst_ref=xbuf.at[section, pl.ds(HB, TR)],
            send_sem=s_main.at[owner],
            recv_sem=r_main.at[section],
            device_id=(owner, gx, gy),
            device_id_type=MESH,
        )

    def strip_copy(owner, section, dx, rows, here=False):
        if dx < 0:
            src, dst = pl.ds(0, rows), pl.ds(HB + TR, rows)
        else:
            src, dst = pl.ds(TR - rows, rows), pl.ds(HB - rows, rows)
        side = (dx + 1) // 2
        return pltpu.make_async_remote_copy(
            src_ref=wbuf.at[owner, src],
            dst_ref=xbuf.at[section, dst],
            send_sem=s_strip.at[NT * side + owner],
            recv_sem=r_strip.at[NT * side + section],
            device_id=(ta, gx, gy) if here else (owner, gx + dx, gy),
            device_id_type=MESH,
        )

    def edge_copy(section, dx, dy, here=False):
        slot, owner = (0, 0) if dy > 0 else (1, NT - 1)
        start, rows = EDGE[dx]
        return pltpu.make_async_remote_copy(
            src_ref=ebuf.at[slot, pl.ds(start, rows)],
            dst_ref=xedge.at[section, pl.ds(start, rows)],
            send_sem=s_edge.at[3 * slot + dx + 1],
            recv_sem=r_edge.at[3 * section + dx + 1],
            device_id=(ta, gx, gy) if here else (ring(lax.rem(owner + NT - ta, NT)), gx + dx, gy + dy),
            device_id_type=MESH,
        )

    def coef_copy(dx, dy, here=False):
        if dy == 0:
            if dx < 0:
                src, dst = pl.ds(HB, RAD), pl.ds(HB + TR, RAD)
            else:
                src, dst = pl.ds(HB + TR - RAD, RAD), pl.ds(HB - RAD, RAD)
            src, dst = cwin.at[:, src, :], cwin.at[:, dst, :]
        else:
            place = pl.ds(*EDGE[dx])
            src, dst = cfold.at[:, place, :], cedge.at[:, place, :]
        at = 3 * (1 if dy else 0) + dx + 1
        return pltpu.make_async_remote_copy(
            src_ref=src,
            dst_ref=dst,
            send_sem=sc.at[at],
            recv_sem=rc.at[at],
            device_id=(ta, gx, gy) if here else (ta, gx + dx, gy + dy),
            device_id_type=MESH,
        )

    coef_dirs = [(-1, 0, None), (1, 0, None)]
    coef_dirs += [(dx, 1, 0) for dx in (-1, 0, 1)] + [(dx, -1, NT - 1) for dx in (-1, 0, 1)]

    def sends(act):
        for dx in (-1, 1, 0):
            for dy in (-1, 1):

                @pl.when(has(dx, dy))
                def _():
                    act(edge_copy(ta, dx, dy))

        for dx, dy, only in coef_dirs:
            near = has(dx, dy)

            @pl.when(near if only is None else near & (ta == only))
            def _():
                act(coef_copy(dx, dy))

        for first, last, rows in ROWS:

            @pl.when((ta >= first) & (ta <= last))
            def _():
                for step in ORDER:
                    for dx in (-1, 1):

                        @pl.when(has(dx, 0))
                        def _():
                            act(strip_copy(mirror(step), ta, dx, rows))

        for step in ORDER[:-1]:
            act(main_copy(mirror(step), ta))

    sends(lambda copy: copy.start())

    for dx, dy, only in coef_dirs:
        near = has(-dx, -dy)

        @pl.when(near if only is None else near & (ta == only))
        def _():
            coef_copy(dx, dy, True).wait_recv()

    cfull[...] = cwin[...]
    edge_lane = lax.broadcasted_iota(jnp.int32, (8, LT), 1)
    for owner, base in ((0, 96), (NT - 1, 0)):

        @pl.when(ta == owner)
        def _():
            mine = (edge_lane >= base) & (edge_lane < base + 32)
            for part in range(3):
                for at, value in unfold(lambda start: cedge[part, start : start + 8], base):
                    rows = slice(8 * at, 8 * at + 8)
                    cfull[part, rows] = jnp.where(mine, value, cfull[part, rows])

    wlane = lax.broadcasted_iota(jnp.int32, (WR, LT), 1)
    row = lax.broadcasted_iota(jnp.int32, (WR, LT), 0)

    def mean(part):
        value = cfull[part]
        value = value + roll(value, -1, 1)
        return value + roll(value, -1, 0)

    stiff = mean(0) * (0.25 * 0.1 / 6.0)
    vx = mean(1) * (0.25 * 0.1 / 8.0)
    vy = mean(2) * (0.25 * 0.1 / 8.0)
    gam = vx + vy
    kap = vx - vy
    column = (
        gy * TC + ta * 64 + jnp.where(
            even,
            jnp.where(wlane < 96, wlane, wlane - LT),
            jnp.where(wlane < 32, wlane + 64, wlane - 64),
        )
    )
    line = gx * TR + row - HB
    inside = (column >= 0) & (column < gyn * TC) & (line >= 0) & (line < gxn * TR)

    def put(slot, shift, value):
        coef[slot] = roll(jnp.where(inside, value, 0.0), shift, 0)

    def before(value):
        return roll(value, 1, 0)

    def left(value):
        return roll(value, 1, 1)

    put(0, 0, (4.0 * stiff - gam) + before(4.0 * stiff + kap) + left(4.0 * stiff - kap + before(4.0 * stiff + gam)))
    put(1, 0, (-stiff - kap) + before(gam - stiff))
    put(2, 0, left((-stiff - gam) + before(kap - stiff)))
    put(3, 1, (kap - stiff) + left(gam - stiff))
    put(4, 1, gam - 2.0 * stiff)
    put(5, 1, left(kap - 2.0 * stiff))
    put(6, -1, before((-stiff - gam) + left(-stiff - kap)))
    put(7, -1, before(-kap - 2.0 * stiff))
    put(8, -1, left(before(-gam - 2.0 * stiff)))

    def rate(value, span):
        start, rows = span
        high = roll(value, -1, 1)
        low = roll(value, 1, 1)

        def line_sum(slot):
            return (
                coef[slot, start : start + rows] * value
                + coef[slot + 1, start : start + rows] * high
                + coef[slot + 2, start : start + rows] * low
            )

        return line_sum(0) + roll(line_sum(3), -1, 0) + roll(line_sum(6), 1, 0)

    def trim(value, old, new):
        skip = new[0] - old[0]
        return value[skip : skip + new[1]]

    def result_copy(section):
        return pltpu.make_async_remote_copy(
            src_ref=fsend.at[section],
            dst_ref=frecv.at[ta],
            send_sem=sf.at[section],
            recv_sem=rf.at[ta],
            device_id=(section, gx, gy),
            device_id_type=MESH,
        )

    flane = lax.broadcasted_iota(jnp.int32, (TR // 2, LT), 1)
    fmain = jnp.where(even, flane, LT - 1 - flane) < 64
    def arrive(section, halo, span):
        @pl.when(ta != section)
        def _():
            main_copy(section, section).wait_recv()

        for dx in (-1, 1):

            @pl.when(has(-dx, 0))
            def _():
                strip_copy(section, section, dx, halo, True).wait_recv()

        for owner, dy, base in ((0, 1, 96), (NT - 1, -1, 0)):

            @pl.when(ta == owner)
            def _():
                for dx in (-1, 0, 1):

                    @pl.when(has(-dx, -dy))
                    def _():
                        edge_copy(section, dx, dy, True).wait_recv()

                mine = (edge_lane >= base) & (edge_lane < base + 32)
                for at, value in unfold(lambda start: xedge[section, start : start + 8], base):
                    if span[0] <= 8 * at < span[0] + span[1]:
                        place = slice(8 * at, 8 * at + 8)
                        xbuf[section, place] = jnp.where(mine, value, xbuf[section, place])

        value = xbuf[section, span[0] : span[0] + span[1]]
        return 0.5 * rate(value - 0.25 * rate(value, span), span)

    def advance(value, half, span):
        return value - 2.0 * rate(value - rate(value - half, span), span)

    def give(section, value, span):
        tile = trim(value, span, (HB, TR))
        fsend[section] = jnp.where(fmain, tile[: TR // 2], roll(tile[TR // 2 :], 64, 1))

        @pl.when(ta != section)
        def _():
            result_copy(section).start()

    inner = slice(SPAN[0], SPAN[0] + SPAN[1])
    last = slice(LAST[0], LAST[0] + LAST[1])
    half[...] = arrive(0, RAD, FULL)
    state[inner] = xbuf[0, inner]

    def step(section, carry, halo, span):
        rows = slice(span[0], span[0] + span[1])
        after = arrive(section, halo, span)
        value = advance(state[rows], half[rows], span)
        state[rows] = value
        half[rows] = after
        give(section - 1, value, span)
        return carry

    lax.fori_loop(1, 5, functools.partial(step, halo=16, span=SPAN), 0)
    lax.fori_loop(5, NT, functools.partial(step, halo=8, span=LAST), 0)
    give(NT - 1, advance(state[last], half[last], LAST), LAST)

    frecv[ta] = fsend[ta]

    sends(lambda copy: copy.wait_send())
    for step in range(1, NT):
        result_copy(lax.rem(ta + step, NT)).wait_send()

    for step in range(1, NT):
        peer = lax.rem(ta + step, NT)
        pltpu.make_async_remote_copy(
            src_ref=fsend.at[peer],
            dst_ref=frecv.at[peer],
            send_sem=sf.at[peer],
            recv_sem=rf.at[peer],
            device_id=(peer, gx, gy),
            device_id_type=MESH,
        ).wait_recv()

    for tile in range(4):
        lower, upper = frecv[2 * tile], frecv[2 * tile + 1]
        lanes = slice(tile * LT, (tile + 1) * LT)
        out_ref[0, : TR // 2, lanes] = jnp.where(flane < 64, lower, upper)
        out_ref[0, TR // 2 :, lanes] = roll(jnp.where(flane < 64, upper, lower), 64, 1)


def solution(mesh):
    gxn, gyn = mesh.shape["gx"], mesh.shape["gy"]

    def local(start_states, conduct, velocity):
        return pl.pallas_call(
            functools.partial(kernel, gxn, gyn),
            out_shape=pltpu.VMEM((1, TR, TC), jnp.float32),
            in_specs=[pl.BlockSpec(memory_space=pl.ANY)] * 3,
            out_specs=pl.BlockSpec(memory_space=pltpu.VMEM),
            scratch_shapes=[
                pltpu.VMEM((TR, TC), jnp.float32),
                pltpu.VMEM((NT, TR, LT), jnp.float32),
                pltpu.VMEM((NT, WR, LT), jnp.float32),
                pltpu.VMEM((2, ER, LT), jnp.float32),
                pltpu.VMEM((NT, ER, LT), jnp.float32),
                pltpu.VMEM((3, TR, LT), jnp.float32),
                pltpu.VMEM((3, TR, LT), jnp.float32),
                pltpu.VMEM((3, WR, LT), jnp.float32),
                pltpu.VMEM((3, WR, LT), jnp.float32),
                pltpu.VMEM((3, ER, LT), jnp.float32),
                pltpu.VMEM((3, ER, LT), jnp.float32),
                pltpu.VMEM((9, WR, LT), jnp.float32),
                pltpu.VMEM((WR, LT), jnp.float32),
                pltpu.VMEM((WR, LT), jnp.float32),
                pltpu.VMEM((NT, TR // 2, LT), jnp.float32),
                pltpu.VMEM((NT, TR // 2, LT), jnp.float32),
                pltpu.SemaphoreType.DMA((5,)),
                pltpu.SemaphoreType.DMA((NT,)),
                pltpu.SemaphoreType.DMA((NT,)),
                pltpu.SemaphoreType.DMA((2 * NT,)),
                pltpu.SemaphoreType.DMA((2 * NT,)),
                pltpu.SemaphoreType.DMA((6,)),
                pltpu.SemaphoreType.DMA((3 * NT,)),
                pltpu.SemaphoreType.DMA((6,)),
                pltpu.SemaphoreType.DMA((6,)),
                pltpu.SemaphoreType.DMA((NT,)),
                pltpu.SemaphoreType.DMA((NT,)),
            ],
            compiler_params=pltpu.CompilerParams(collective_id=0, has_side_effects=True),
        )(start_states, conduct, velocity)

    in_specs = (P("ta", "gx", "gy"), P("gx", "gy"), P(None, "gx", "gy"))
    return jax.shard_map(
        local, mesh=mesh, in_specs=in_specs, out_specs=P("ta", "gx", "gy"), check_vma=False
    )
```

```python
import functools

import jax
import jax.numpy as jnp
from jax import lax
from jax.experimental import pallas as pl
from jax.experimental.pallas import tpu as pltpu
from jax.sharding import PartitionSpec as P

MESH = pl.DeviceIdType.MESH
NT = 8
TR = 64
TC = 512
LT = 128
HB = 24
RAD = 18
ORDER = (5, 4, 3, 7, 2, 6, 1, 0)
WR = TR + 2 * HB
ER = 32
ROWS = [(0, 0, RAD), (1, 4, 16), (5, 7, 8)]
FULL = (0, WR)
SPAN = (8, WR - 16)
LAST = (16, WR - 32)
EDGE = {1: (0, 8), 0: (8, 16), -1: (24, 8)}


def roll(value, shift, axis):
    return pltpu.roll(value, shift % value.shape[axis], axis)


def fold(read, base):
    lane = lax.broadcasted_iota(jnp.int32, (8, LT), 1)
    parts = []
    for start, groups in ((40, 3), (0, 4), (32, 4), (0, 3)):
        value = roll(read(start), base, 1)
        for group in range(1, groups):
            moved = roll(read(start + 8 * group), base + 32 * group, 1)
            value = jnp.where(lane < 32 * group, value, moved)
        parts.append(value)
    return parts


def unfold(read, base):
    for start, groups, first in ((0, 3, 0), (8, 4, 3), (16, 4, 7), (24, 3, 11)):
        value = read(start)
        for group in range(groups):
            yield first + group, roll(value, base - 32 * group, 1)


def kernel(
    gxn, gyn, u_ref, cond_ref, vel_ref, out_ref,
    ubuf, wbuf, xbuf, ebuf, xedge, main, other, cwin, cfull, cfold, cedge, coef, state, half, fsend, frecv,
    load_sem, s_main, r_main, s_strip, r_strip, s_edge, r_edge, sc, rc, sf, rf,
):
    ta = lax.axis_index("ta")
    gx = lax.axis_index("gx")
    gy = lax.axis_index("gy")
    even = lax.rem(ta, 2) == 0
    tile_m = ta // 2
    tile_o = lax.rem(tile_m + jnp.where(even, 3, 1), 4)

    def has(dx, dy):
        x, y = gx + dx, gy + dy
        return (x >= 0) & (x < gxn) & (y >= 0) & (y < gyn)

    def ring(step):
        return lax.rem(ta + step, NT)

    def mirror(step):
        return ring(jnp.where(even, step, NT - step))

    barrier = pltpu.get_barrier_semaphore()

    def greet(section, dx, dy):
        pl.semaphore_signal(
            barrier, inc=1, device_id=(section, gx + dx, gy + dy), device_id_type=MESH
        )

    for dx in (-1, 1):

        @pl.when(has(dx, 0))
        def _():
            for step in range(NT):
                greet(ring(step), dx, 0)

    for owner, dy in ((0, -1), (NT - 1, 1)):
        for dx in (-1, 0, 1):

            @pl.when((ta == owner) & has(dx, dy))
            def _():
                for step in range(NT):
                    greet(ring(step), dx, dy)

    for step in range(1, NT):
        greet(ring(step), 0, 0)

    lanes_m = pl.ds(pl.multiple_of(tile_m * LT, LT), LT)
    lanes_o = pl.ds(pl.multiple_of(tile_o * LT, LT), LT)
    loads = [
        pltpu.make_async_copy(u_ref.at[0], ubuf, load_sem.at[0]),
        pltpu.make_async_copy(cond_ref.at[:, lanes_m], main.at[0], load_sem.at[1]),
        pltpu.make_async_copy(cond_ref.at[:, lanes_o], other.at[0], load_sem.at[2]),
        pltpu.make_async_copy(vel_ref.at[:, :, lanes_m], main.at[pl.ds(1, 2)], load_sem.at[3]),
        pltpu.make_async_copy(vel_ref.at[:, :, lanes_o], other.at[pl.ds(1, 2)], load_sem.at[4]),
    ]
    for load in loads:
        load.start()

    count = NT - 1
    for dx in (-1, 1):
        count = count + NT * has(dx, 0).astype(jnp.int32)
    for dy in (-1, 1):
        for dx in (-1, 0, 1):
            count = count + has(dx, dy).astype(jnp.int32)

    xbuf[0, 0:6, :] = jnp.zeros((6, LT), jnp.float32)
    xbuf[0, WR - 6 : WR, :] = jnp.zeros((6, LT), jnp.float32)
    cwin[:, 0:6, :] = jnp.zeros((3, 6, LT), jnp.float32)
    cwin[:, WR - 6 : WR, :] = jnp.zeros((3, 6, LT), jnp.float32)

    def clear(ref, planes, start, rows):
        ref[:, start : start + rows, :] = jnp.zeros((planes, rows, LT), jnp.float32)

    for dx, start in ((1, 0), (-1, HB + TR)):

        @pl.when(jnp.logical_not(has(-dx, 0)))
        def _():
            clear(xbuf, NT, start, HB)
            clear(cwin, 3, start, HB)

    for owner, dy in ((0, 1), (NT - 1, -1)):
        for dx in (-1, 0, 1):

            @pl.when((ta == owner) & jnp.logical_not(has(-dx, -dy)))
            def _():
                clear(xedge, NT, *EDGE[dx])
                clear(cedge, 3, *EDGE[dx])

    for load in loads:
        load.wait()

    lane = lax.broadcasted_iota(jnp.int32, (TR, LT), 1)
    for owner in range(NT):
        tile = owner // 2
        if owner % 2 == 0:
            mate, keep = (tile + 3) % 4, lane < 96
        else:
            mate, keep = (tile + 1) % 4, lane >= 32
        wbuf[owner] = jnp.where(
            keep, ubuf[:, tile * LT : (tile + 1) * LT], ubuf[:, mate * LT : (mate + 1) * LT]
        )
    for slot, (first, base) in enumerate(((3 * LT, 32), (0, 0))):
        for at, part in enumerate(fold(lambda start: ubuf[start : start + 8, first : first + LT], base)):
            ebuf[slot, 8 * at : 8 * at + 8] = part
    use_m = jnp.where(even, lane, LT - 1 - lane) < 96
    for part in range(3):
        cwin[part, HB : HB + TR, :] = jnp.where(use_m, main[part], other[part])
    for owner, base in ((0, 32), (NT - 1, 0)):

        @pl.when(ta == owner)
        def _():
            for part in range(3):
                for at, value in enumerate(fold(lambda start: other[part, start : start + 8], base)):
                    cfold[part, 8 * at : 8 * at + 8] = value

    xbuf[ta, HB : HB + TR] = wbuf[ta]
    pl.semaphore_wait(barrier, count)

    def main_copy(owner, section):
        return pltpu.make_async_remote_copy(
            src_ref=wbuf.at[owner],
            dst_ref=xbuf.at[section, pl.ds(HB, TR)],
            send_sem=s_main.at[owner],
            recv_sem=r_main.at[section],
            device_id=(owner, gx, gy),
            device_id_type=MESH,
        )

    def strip_copy(owner, section, dx, rows, here=False):
        if dx < 0:
            src, dst = pl.ds(0, rows), pl.ds(HB + TR, rows)
        else:
            src, dst = pl.ds(TR - rows, rows), pl.ds(HB - rows, rows)
        side = (dx + 1) // 2
        return pltpu.make_async_remote_copy(
            src_ref=wbuf.at[owner, src],
            dst_ref=xbuf.at[section, dst],
            send_sem=s_strip.at[NT * side + owner],
            recv_sem=r_strip.at[NT * side + section],
            device_id=(ta, gx, gy) if here else (owner, gx + dx, gy),
            device_id_type=MESH,
        )

    def edge_copy(section, dx, dy, here=False):
        slot, owner = (0, 0) if dy > 0 else (1, NT - 1)
        start, rows = EDGE[dx]
        return pltpu.make_async_remote_copy(
            src_ref=ebuf.at[slot, pl.ds(start, rows)],
            dst_ref=xedge.at[section, pl.ds(start, rows)],
            send_sem=s_edge.at[3 * slot + dx + 1],
            recv_sem=r_edge.at[3 * section + dx + 1],
            device_id=(ta, gx, gy) if here else (ring(lax.rem(owner + NT - ta, NT)), gx + dx, gy + dy),
            device_id_type=MESH,
        )

    def coef_copy(dx, dy, here=False):
        if dy == 0:
            if dx < 0:
                src, dst = pl.ds(HB, RAD), pl.ds(HB + TR, RAD)
            else:
                src, dst = pl.ds(HB + TR - RAD, RAD), pl.ds(HB - RAD, RAD)
            src, dst = cwin.at[:, src, :], cwin.at[:, dst, :]
        else:
            place = pl.ds(*EDGE[dx])
            src, dst = cfold.at[:, place, :], cedge.at[:, place, :]
        at = 3 * (1 if dy else 0) + dx + 1
        return pltpu.make_async_remote_copy(
            src_ref=src,
            dst_ref=dst,
            send_sem=sc.at[at],
            recv_sem=rc.at[at],
            device_id=(ta, gx, gy) if here else (ta, gx + dx, gy + dy),
            device_id_type=MESH,
        )

    coef_dirs = [(-1, 0, None), (1, 0, None)]
    coef_dirs += [(dx, 1, 0) for dx in (-1, 0, 1)] + [(dx, -1, NT - 1) for dx in (-1, 0, 1)]

    def sends(act):
        for dx in (-1, 1, 0):
            for dy in (-1, 1):

                @pl.when(has(dx, dy))
                def _():
                    act(edge_copy(ta, dx, dy))

        for first, last, rows in ROWS:

            @pl.when((ta >= first) & (ta <= last))
            def _():
                for step in ORDER:
                    for dx in (-1, 1):

                        @pl.when(has(dx, 0))
                        def _():
                            act(strip_copy(mirror(step), ta, dx, rows))

        for dx, dy, only in coef_dirs:
            near = has(dx, dy)

            @pl.when(near if only is None else near & (ta == only))
            def _():
                act(coef_copy(dx, dy))

        for step in ORDER[:-1]:
            act(main_copy(mirror(step), ta))

    sends(lambda copy: copy.start())

    for dx, dy, only in coef_dirs:
        near = has(-dx, -dy)

        @pl.when(near if only is None else near & (ta == only))
        def _():
            coef_copy(dx, dy, True).wait_recv()

    cfull[...] = cwin[...]
    edge_lane = lax.broadcasted_iota(jnp.int32, (8, LT), 1)
    for owner, base in ((0, 96), (NT - 1, 0)):

        @pl.when(ta == owner)
        def _():
            mine = (edge_lane >= base) & (edge_lane < base + 32)
            for part in range(3):
                for at, value in unfold(lambda start: cedge[part, start : start + 8], base):
                    rows = slice(8 * at, 8 * at + 8)
                    cfull[part, rows] = jnp.where(mine, value, cfull[part, rows])

    wlane = lax.broadcasted_iota(jnp.int32, (WR, LT), 1)
    row = lax.broadcasted_iota(jnp.int32, (WR, LT), 0)

    def mean(part):
        value = cfull[part]
        value = value + roll(value, -1, 1)
        return value + roll(value, -1, 0)

    stiff = mean(0) * (0.25 * 0.1 / 6.0)
    vx = mean(1) * (0.25 * 0.1 / 8.0)
    vy = mean(2) * (0.25 * 0.1 / 8.0)
    gam = vx + vy
    kap = vx - vy
    column = (
        gy * TC + ta * 64 + jnp.where(
            even,
            jnp.where(wlane < 96, wlane, wlane - LT),
            jnp.where(wlane < 32, wlane + 64, wlane - 64),
        )
    )
    line = gx * TR + row - HB
    inside = (column >= 0) & (column < gyn * TC) & (line >= 0) & (line < gxn * TR)

    def put(slot, shift, value):
        coef[slot] = roll(jnp.where(inside, value, 0.0), shift, 0)

    def before(value):
        return roll(value, 1, 0)

    def left(value):
        return roll(value, 1, 1)

    put(0, 0, (4.0 * stiff - gam) + before(4.0 * stiff + kap) + left(4.0 * stiff - kap + before(4.0 * stiff + gam)))
    put(1, 0, (-stiff - kap) + before(gam - stiff))
    put(2, 0, left((-stiff - gam) + before(kap - stiff)))
    put(3, 1, (kap - stiff) + left(gam - stiff))
    put(4, 1, gam - 2.0 * stiff)
    put(5, 1, left(kap - 2.0 * stiff))
    put(6, -1, before((-stiff - gam) + left(-stiff - kap)))
    put(7, -1, before(-kap - 2.0 * stiff))
    put(8, -1, left(before(-gam - 2.0 * stiff)))

    def rate(value, span):
        start, rows = span
        high = roll(value, -1, 1)
        low = roll(value, 1, 1)

        def line_sum(slot):
            return (
                coef[slot, start : start + rows] * value
                + coef[slot + 1, start : start + rows] * high
                + coef[slot + 2, start : start + rows] * low
            )

        return line_sum(0) + roll(line_sum(3), -1, 0) + roll(line_sum(6), 1, 0)

    def trim(value, old, new):
        skip = new[0] - old[0]
        return value[skip : skip + new[1]]

    def result_copy(section):
        return pltpu.make_async_remote_copy(
            src_ref=fsend.at[section],
            dst_ref=frecv.at[ta],
            send_sem=sf.at[section],
            recv_sem=rf.at[ta],
            device_id=(section, gx, gy),
            device_id_type=MESH,
        )

    flane = lax.broadcasted_iota(jnp.int32, (TR // 2, LT), 1)
    fmain = jnp.where(even, flane, LT - 1 - flane) < 64
    def arrive(section, halo, span):
        @pl.when(ta != section)
        def _():
            main_copy(section, section).wait_recv()

        for dx in (-1, 1):

            @pl.when(has(-dx, 0))
            def _():
                strip_copy(section, section, dx, halo, True).wait_recv()

        for owner, dy, base in ((0, 1, 96), (NT - 1, -1, 0)):

            @pl.when(ta == owner)
            def _():
                for dx in (-1, 0, 1):

                    @pl.when(has(-dx, -dy))
                    def _():
                        edge_copy(section, dx, dy, True).wait_recv()

                mine = (edge_lane >= base) & (edge_lane < base + 32)
                for at, value in unfold(lambda start: xedge[section, start : start + 8], base):
                    if span[0] <= 8 * at < span[0] + span[1]:
                        place = slice(8 * at, 8 * at + 8)
                        xbuf[section, place] = jnp.where(mine, value, xbuf[section, place])

        value = xbuf[section, span[0] : span[0] + span[1]]
        return 0.5 * rate(value - 0.25 * rate(value, span), span)

    def advance(value, half, span):
        return value - 2.0 * rate(value - rate(value - half, span), span)

    def give(section, value, span):
        tile = trim(value, span, (HB, TR))
        fsend[section] = jnp.where(fmain, tile[: TR // 2], roll(tile[TR // 2 :], 64, 1))

        @pl.when(ta != section)
        def _():
            result_copy(section).start()

    inner = slice(SPAN[0], SPAN[0] + SPAN[1])
    last = slice(LAST[0], LAST[0] + LAST[1])
    half[...] = arrive(0, RAD, FULL)
    state[inner] = xbuf[0, inner]

    def step(section, carry, halo, span):
        rows = slice(span[0], span[0] + span[1])
        after = arrive(section, halo, span)
        value = advance(state[rows], half[rows], span)
        state[rows] = value
        half[rows] = after
        give(section - 1, value, span)
        return carry

    lax.fori_loop(1, 5, functools.partial(step, halo=16, span=SPAN), 0)
    lax.fori_loop(5, NT, functools.partial(step, halo=8, span=LAST), 0)
    give(NT - 1, advance(state[last], half[last], LAST), LAST)

    frecv[ta] = fsend[ta]

    sends(lambda copy: copy.wait_send())
    for step in range(1, NT):
        result_copy(lax.rem(ta + step, NT)).wait_send()

    for step in range(1, NT):
        peer = lax.rem(ta + step, NT)
        pltpu.make_async_remote_copy(
            src_ref=fsend.at[peer],
            dst_ref=frecv.at[peer],
            send_sem=sf.at[peer],
            recv_sem=rf.at[peer],
            device_id=(peer, gx, gy),
            device_id_type=MESH,
        ).wait_recv()

    for tile in range(4):
        lower, upper = frecv[2 * tile], frecv[2 * tile + 1]
        lanes = slice(tile * LT, (tile + 1) * LT)
        out_ref[0, : TR // 2, lanes] = jnp.where(flane < 64, lower, upper)
        out_ref[0, TR // 2 :, lanes] = roll(jnp.where(flane < 64, upper, lower), 64, 1)


def solution(mesh):
    gxn, gyn = mesh.shape["gx"], mesh.shape["gy"]

    def local(start_states, conduct, velocity):
        return pl.pallas_call(
            functools.partial(kernel, gxn, gyn),
            out_shape=pltpu.VMEM((1, TR, TC), jnp.float32),
            in_specs=[pl.BlockSpec(memory_space=pl.ANY)] * 3,
            out_specs=pl.BlockSpec(memory_space=pltpu.VMEM),
            scratch_shapes=[
                pltpu.VMEM((TR, TC), jnp.float32),
                pltpu.VMEM((NT, TR, LT), jnp.float32),
                pltpu.VMEM((NT, WR, LT), jnp.float32),
                pltpu.VMEM((2, ER, LT), jnp.float32),
                pltpu.VMEM((NT, ER, LT), jnp.float32),
                pltpu.VMEM((3, TR, LT), jnp.float32),
                pltpu.VMEM((3, TR, LT), jnp.float32),
                pltpu.VMEM((3, WR, LT), jnp.float32),
                pltpu.VMEM((3, WR, LT), jnp.float32),
                pltpu.VMEM((3, ER, LT), jnp.float32),
                pltpu.VMEM((3, ER, LT), jnp.float32),
                pltpu.VMEM((9, WR, LT), jnp.float32),
                pltpu.VMEM((WR, LT), jnp.float32),
                pltpu.VMEM((WR, LT), jnp.float32),
                pltpu.VMEM((NT, TR // 2, LT), jnp.float32),
                pltpu.VMEM((NT, TR // 2, LT), jnp.float32),
                pltpu.SemaphoreType.DMA((5,)),
                pltpu.SemaphoreType.DMA((NT,)),
                pltpu.SemaphoreType.DMA((NT,)),
                pltpu.SemaphoreType.DMA((2 * NT,)),
                pltpu.SemaphoreType.DMA((2 * NT,)),
                pltpu.SemaphoreType.DMA((6,)),
                pltpu.SemaphoreType.DMA((3 * NT,)),
                pltpu.SemaphoreType.DMA((6,)),
                pltpu.SemaphoreType.DMA((6,)),
                pltpu.SemaphoreType.DMA((NT,)),
                pltpu.SemaphoreType.DMA((NT,)),
            ],
            compiler_params=pltpu.CompilerParams(collective_id=0, has_side_effects=True),
        )(start_states, conduct, velocity)

    in_specs = (P("ta", "gx", "gy"), P("gx", "gy"), P(None, "gx", "gy"))
    return jax.shard_map(
        local, mesh=mesh, in_specs=in_specs, out_specs=P("ta", "gx", "gy"), check_vma=False
    )
```

```python
import functools

import jax
import jax.numpy as jnp
from jax import lax
from jax.experimental import pallas as pl
from jax.experimental.pallas import tpu as pltpu
from jax.sharding import PartitionSpec as P

MESH = pl.DeviceIdType.MESH
NT = 8
TR = 64
TC = 512
LT = 128
HB = 24
RAD = 18
ORDER = (5, 4, 3, 7, 2, 6, 1, 0)
WR = TR + 2 * HB
ER = 32
ROWS = [(0, 0, RAD), (1, 4, 16), (5, 7, 8)]
FULL = (0, WR)
SPAN = (8, WR - 16)
LAST = (16, WR - 32)
EDGE = {1: (0, 8), 0: (8, 16), -1: (24, 8)}


def roll(value, shift, axis):
    return pltpu.roll(value, shift % value.shape[axis], axis)


def fold(read, base):
    lane = lax.broadcasted_iota(jnp.int32, (8, LT), 1)
    parts = []
    for start, groups in ((40, 3), (0, 4), (32, 4), (0, 3)):
        value = roll(read(start), base, 1)
        for group in range(1, groups):
            moved = roll(read(start + 8 * group), base + 32 * group, 1)
            value = jnp.where(lane < 32 * group, value, moved)
        parts.append(value)
    return parts


def unfold(read, base):
    for start, groups, first in ((0, 3, 0), (8, 4, 3), (16, 4, 7), (24, 3, 11)):
        value = read(start)
        for group in range(groups):
            yield first + group, roll(value, base - 32 * group, 1)


def kernel(
    gxn, gyn, u_ref, cond_ref, vel_ref, out_ref,
    ubuf, wbuf, xbuf, ebuf, xedge, main, other, cwin, cfull, cfold, cedge, coef, state, half, fsend, frecv,
    load_sem, s_main, r_main, s_strip, r_strip, s_edge, r_edge, sc, rc, sf, rf,
):
    ta = lax.axis_index("ta")
    gx = lax.axis_index("gx")
    gy = lax.axis_index("gy")
    even = lax.rem(ta, 2) == 0
    tile_m = ta // 2
    tile_o = lax.rem(tile_m + jnp.where(even, 3, 1), 4)

    def has(dx, dy):
        x, y = gx + dx, gy + dy
        return (x >= 0) & (x < gxn) & (y >= 0) & (y < gyn)

    def ring(step):
        return lax.rem(ta + step, NT)

    def mirror(step):
        return ring(jnp.where(even, step, NT - step))

    barrier = pltpu.get_barrier_semaphore()

    def greet(section, dx, dy):
        pl.semaphore_signal(
            barrier, inc=1, device_id=(section, gx + dx, gy + dy), device_id_type=MESH
        )

    for dx in (-1, 1):

        @pl.when(has(dx, 0))
        def _():
            for step in range(NT):
                greet(ring(step), dx, 0)

    for owner, dy in ((0, -1), (NT - 1, 1)):
        for dx in (-1, 0, 1):

            @pl.when((ta == owner) & has(dx, dy))
            def _():
                for step in range(NT):
                    greet(ring(step), dx, dy)

    for step in range(1, NT):
        greet(ring(step), 0, 0)

    lanes_m = pl.ds(pl.multiple_of(tile_m * LT, LT), LT)
    lanes_o = pl.ds(pl.multiple_of(tile_o * LT, LT), LT)
    loads = [
        pltpu.make_async_copy(u_ref.at[0], ubuf, load_sem.at[0]),
        pltpu.make_async_copy(cond_ref.at[:, lanes_m], main.at[0], load_sem.at[1]),
        pltpu.make_async_copy(cond_ref.at[:, lanes_o], other.at[0], load_sem.at[2]),
        pltpu.make_async_copy(vel_ref.at[:, :, lanes_m], main.at[pl.ds(1, 2)], load_sem.at[3]),
        pltpu.make_async_copy(vel_ref.at[:, :, lanes_o], other.at[pl.ds(1, 2)], load_sem.at[4]),
    ]
    for load in loads:
        load.start()

    count = NT - 1
    for dx in (-1, 1):
        count = count + NT * has(dx, 0).astype(jnp.int32)
    for dy in (-1, 1):
        for dx in (-1, 0, 1):
            count = count + has(dx, dy).astype(jnp.int32)

    xbuf[0, 0:6, :] = jnp.zeros((6, LT), jnp.float32)
    xbuf[0, WR - 6 : WR, :] = jnp.zeros((6, LT), jnp.float32)
    cwin[:, 0:6, :] = jnp.zeros((3, 6, LT), jnp.float32)
    cwin[:, WR - 6 : WR, :] = jnp.zeros((3, 6, LT), jnp.float32)

    def clear(ref, planes, start, rows):
        ref[:, start : start + rows, :] = jnp.zeros((planes, rows, LT), jnp.float32)

    for dx, start in ((1, 0), (-1, HB + TR)):

        @pl.when(jnp.logical_not(has(-dx, 0)))
        def _():
            clear(xbuf, NT, start, HB)
            clear(cwin, 3, start, HB)

    for owner, dy in ((0, 1), (NT - 1, -1)):
        for dx in (-1, 0, 1):

            @pl.when((ta == owner) & jnp.logical_not(has(-dx, -dy)))
            def _():
                clear(xedge, NT, *EDGE[dx])
                clear(cedge, 3, *EDGE[dx])

    for load in loads:
        load.wait()

    lane = lax.broadcasted_iota(jnp.int32, (TR, LT), 1)
    for owner in range(NT):
        tile = owner // 2
        if owner % 2 == 0:
            mate, keep = (tile + 3) % 4, lane < 96
        else:
            mate, keep = (tile + 1) % 4, lane >= 32
        wbuf[owner] = jnp.where(
            keep, ubuf[:, tile * LT : (tile + 1) * LT], ubuf[:, mate * LT : (mate + 1) * LT]
        )
    for slot, (first, base) in enumerate(((3 * LT, 32), (0, 0))):
        for at, part in enumerate(fold(lambda start: ubuf[start : start + 8, first : first + LT], base)):
            ebuf[slot, 8 * at : 8 * at + 8] = part
    use_m = jnp.where(even, lane, LT - 1 - lane) < 96
    for part in range(3):
        cwin[part, HB : HB + TR, :] = jnp.where(use_m, main[part], other[part])
    for owner, base in ((0, 32), (NT - 1, 0)):

        @pl.when(ta == owner)
        def _():
            for part in range(3):
                for at, value in enumerate(fold(lambda start: other[part, start : start + 8], base)):
                    cfold[part, 8 * at : 8 * at + 8] = value

    xbuf[ta, HB : HB + TR] = wbuf[ta]
    pl.semaphore_wait(barrier, count)

    def main_copy(owner, section):
        return pltpu.make_async_remote_copy(
            src_ref=wbuf.at[owner],
            dst_ref=xbuf.at[section, pl.ds(HB, TR)],
            send_sem=s_main.at[owner],
            recv_sem=r_main.at[section],
            device_id=(owner, gx, gy),
            device_id_type=MESH,
        )

    def strip_copy(owner, section, dx, rows, here=False):
        if dx < 0:
            src, dst = pl.ds(0, rows), pl.ds(HB + TR, rows)
        else:
            src, dst = pl.ds(TR - rows, rows), pl.ds(HB - rows, rows)
        side = (dx + 1) // 2
        return pltpu.make_async_remote_copy(
            src_ref=wbuf.at[owner, src],
            dst_ref=xbuf.at[section, dst],
            send_sem=s_strip.at[NT * side + owner],
            recv_sem=r_strip.at[NT * side + section],
            device_id=(ta, gx, gy) if here else (owner, gx + dx, gy),
            device_id_type=MESH,
        )

    def edge_copy(section, dx, dy, here=False):
        slot, owner = (0, 0) if dy > 0 else (1, NT - 1)
        start, rows = EDGE[dx]
        return pltpu.make_async_remote_copy(
            src_ref=ebuf.at[slot, pl.ds(start, rows)],
            dst_ref=xedge.at[section, pl.ds(start, rows)],
            send_sem=s_edge.at[3 * slot + dx + 1],
            recv_sem=r_edge.at[3 * section + dx + 1],
            device_id=(ta, gx, gy) if here else (ring(lax.rem(owner + NT - ta, NT)), gx + dx, gy + dy),
            device_id_type=MESH,
        )

    def coef_copy(dx, dy, here=False):
        if dy == 0:
            if dx < 0:
                src, dst = pl.ds(HB, RAD), pl.ds(HB + TR, RAD)
            else:
                src, dst = pl.ds(HB + TR - RAD, RAD), pl.ds(HB - RAD, RAD)
            src, dst = cwin.at[:, src, :], cwin.at[:, dst, :]
        else:
            place = pl.ds(*EDGE[dx])
            src, dst = cfold.at[:, place, :], cedge.at[:, place, :]
        at = 3 * (1 if dy else 0) + dx + 1
        return pltpu.make_async_remote_copy(
            src_ref=src,
            dst_ref=dst,
            send_sem=sc.at[at],
            recv_sem=rc.at[at],
            device_id=(ta, gx, gy) if here else (ta, gx + dx, gy + dy),
            device_id_type=MESH,
        )

    coef_dirs = [(-1, 0, None), (1, 0, None)]
    coef_dirs += [(dx, 1, 0) for dx in (-1, 0, 1)] + [(dx, -1, NT - 1) for dx in (-1, 0, 1)]

    def sends(act):
        for dx in (-1, 1, 0):
            for dy in (-1, 1):

                @pl.when(has(dx, dy))
                def _():
                    act(edge_copy(ta, dx, dy))

        for first, last, rows in ROWS:

            @pl.when((ta >= first) & (ta <= last))
            def _():
                for step in ORDER:
                    for dx in (-1, 1):

                        @pl.when(has(dx, 0))
                        def _():
                            act(strip_copy(mirror(step), ta, dx, rows))

        for dx, dy, only in coef_dirs:
            near = has(dx, dy)

            @pl.when(near if only is None else near & (ta == only))
            def _():
                act(coef_copy(dx, dy))

        for step in (4, 5, 3, 7, 2, 6, 1):
            act(main_copy(mirror(step), ta))

    sends(lambda copy: copy.start())

    for dx, dy, only in coef_dirs:
        near = has(-dx, -dy)

        @pl.when(near if only is None else near & (ta == only))
        def _():
            coef_copy(dx, dy, True).wait_recv()

    cfull[...] = cwin[...]
    edge_lane = lax.broadcasted_iota(jnp.int32, (8, LT), 1)
    for owner, base in ((0, 96), (NT - 1, 0)):

        @pl.when(ta == owner)
        def _():
            mine = (edge_lane >= base) & (edge_lane < base + 32)
            for part in range(3):
                for at, value in unfold(lambda start: cedge[part, start : start + 8], base):
                    rows = slice(8 * at, 8 * at + 8)
                    cfull[part, rows] = jnp.where(mine, value, cfull[part, rows])

    wlane = lax.broadcasted_iota(jnp.int32, (WR, LT), 1)
    row = lax.broadcasted_iota(jnp.int32, (WR, LT), 0)

    def mean(part):
        value = cfull[part]
        value = value + roll(value, -1, 1)
        return value + roll(value, -1, 0)

    stiff = mean(0) * (0.25 * 0.1 / 6.0)
    vx = mean(1) * (0.25 * 0.1 / 8.0)
    vy = mean(2) * (0.25 * 0.1 / 8.0)
    gam = vx + vy
    kap = vx - vy
    column = (
        gy * TC + ta * 64 + jnp.where(
            even,
            jnp.where(wlane < 96, wlane, wlane - LT),
            jnp.where(wlane < 32, wlane + 64, wlane - 64),
        )
    )
    line = gx * TR + row - HB
    inside = (column >= 0) & (column < gyn * TC) & (line >= 0) & (line < gxn * TR)

    def put(slot, shift, value):
        coef[slot] = roll(jnp.where(inside, value, 0.0), shift, 0)

    def before(value):
        return roll(value, 1, 0)

    def left(value):
        return roll(value, 1, 1)

    put(0, 0, (4.0 * stiff - gam) + before(4.0 * stiff + kap) + left(4.0 * stiff - kap + before(4.0 * stiff + gam)))
    put(1, 0, (-stiff - kap) + before(gam - stiff))
    put(2, 0, left((-stiff - gam) + before(kap - stiff)))
    put(3, 1, (kap - stiff) + left(gam - stiff))
    put(4, 1, gam - 2.0 * stiff)
    put(5, 1, left(kap - 2.0 * stiff))
    put(6, -1, before((-stiff - gam) + left(-stiff - kap)))
    put(7, -1, before(-kap - 2.0 * stiff))
    put(8, -1, left(before(-gam - 2.0 * stiff)))

    def rate(value, span):
        start, rows = span
        high = roll(value, -1, 1)
        low = roll(value, 1, 1)

        def line_sum(slot):
            return (
                coef[slot, start : start + rows] * value
                + coef[slot + 1, start : start + rows] * high
                + coef[slot + 2, start : start + rows] * low
            )

        return line_sum(0) + roll(line_sum(3), -1, 0) + roll(line_sum(6), 1, 0)

    def trim(value, old, new):
        skip = new[0] - old[0]
        return value[skip : skip + new[1]]

    def result_copy(section):
        return pltpu.make_async_remote_copy(
            src_ref=fsend.at[section],
            dst_ref=frecv.at[ta],
            send_sem=sf.at[section],
            recv_sem=rf.at[ta],
            device_id=(section, gx, gy),
            device_id_type=MESH,
        )

    flane = lax.broadcasted_iota(jnp.int32, (TR // 2, LT), 1)
    fmain = jnp.where(even, flane, LT - 1 - flane) < 64
    def arrive(section, halo, span):
        @pl.when(ta != section)
        def _():
            main_copy(section, section).wait_recv()

        for dx in (-1, 1):

            @pl.when(has(-dx, 0))
            def _():
                strip_copy(section, section, dx, halo, True).wait_recv()

        for owner, dy, base in ((0, 1, 96), (NT - 1, -1, 0)):

            @pl.when(ta == owner)
            def _():
                for dx in (-1, 0, 1):

                    @pl.when(has(-dx, -dy))
                    def _():
                        edge_copy(section, dx, dy, True).wait_recv()

                mine = (edge_lane >= base) & (edge_lane < base + 32)
                for at, value in unfold(lambda start: xedge[section, start : start + 8], base):
                    if span[0] <= 8 * at < span[0] + span[1]:
                        place = slice(8 * at, 8 * at + 8)
                        xbuf[section, place] = jnp.where(mine, value, xbuf[section, place])

        value = xbuf[section, span[0] : span[0] + span[1]]
        return 0.5 * rate(value - 0.25 * rate(value, span), span)

    def advance(value, half, span):
        return value - 2.0 * rate(value - rate(value - half, span), span)

    def give(section, value, span):
        tile = trim(value, span, (HB, TR))
        fsend[section] = jnp.where(fmain, tile[: TR // 2], roll(tile[TR // 2 :], 64, 1))

        @pl.when(ta != section)
        def _():
            result_copy(section).start()

    inner = slice(SPAN[0], SPAN[0] + SPAN[1])
    last = slice(LAST[0], LAST[0] + LAST[1])
    half[...] = arrive(0, RAD, FULL)
    state[inner] = xbuf[0, inner]

    def step(section, carry, halo, span):
        rows = slice(span[0], span[0] + span[1])
        after = arrive(section, halo, span)
        value = advance(state[rows], half[rows], span)
        state[rows] = value
        half[rows] = after
        give(section - 1, value, span)
        return carry

    lax.fori_loop(1, 5, functools.partial(step, halo=16, span=SPAN), 0)
    lax.fori_loop(5, NT, functools.partial(step, halo=8, span=LAST), 0)
    give(NT - 1, advance(state[last], half[last], LAST), LAST)

    frecv[ta] = fsend[ta]

    sends(lambda copy: copy.wait_send())
    for step in range(1, NT):
        result_copy(lax.rem(ta + step, NT)).wait_send()

    for step in range(1, NT):
        peer = lax.rem(ta + step, NT)
        pltpu.make_async_remote_copy(
            src_ref=fsend.at[peer],
            dst_ref=frecv.at[peer],
            send_sem=sf.at[peer],
            recv_sem=rf.at[peer],
            device_id=(peer, gx, gy),
            device_id_type=MESH,
        ).wait_recv()

    for tile in range(4):
        lower, upper = frecv[2 * tile], frecv[2 * tile + 1]
        lanes = slice(tile * LT, (tile + 1) * LT)
        out_ref[0, : TR // 2, lanes] = jnp.where(flane < 64, lower, upper)
        out_ref[0, TR // 2 :, lanes] = roll(jnp.where(flane < 64, upper, lower), 64, 1)


def solution(mesh):
    gxn, gyn = mesh.shape["gx"], mesh.shape["gy"]

    def local(start_states, conduct, velocity):
        return pl.pallas_call(
            functools.partial(kernel, gxn, gyn),
            out_shape=pltpu.VMEM((1, TR, TC), jnp.float32),
            in_specs=[pl.BlockSpec(memory_space=pl.ANY)] * 3,
            out_specs=pl.BlockSpec(memory_space=pltpu.VMEM),
            scratch_shapes=[
                pltpu.VMEM((TR, TC), jnp.float32),
                pltpu.VMEM((NT, TR, LT), jnp.float32),
                pltpu.VMEM((NT, WR, LT), jnp.float32),
                pltpu.VMEM((2, ER, LT), jnp.float32),
                pltpu.VMEM((NT, ER, LT), jnp.float32),
                pltpu.VMEM((3, TR, LT), jnp.float32),
                pltpu.VMEM((3, TR, LT), jnp.float32),
                pltpu.VMEM((3, WR, LT), jnp.float32),
                pltpu.VMEM((3, WR, LT), jnp.float32),
                pltpu.VMEM((3, ER, LT), jnp.float32),
                pltpu.VMEM((3, ER, LT), jnp.float32),
                pltpu.VMEM((9, WR, LT), jnp.float32),
                pltpu.VMEM((WR, LT), jnp.float32),
                pltpu.VMEM((WR, LT), jnp.float32),
                pltpu.VMEM((NT, TR // 2, LT), jnp.float32),
                pltpu.VMEM((NT, TR // 2, LT), jnp.float32),
                pltpu.SemaphoreType.DMA((5,)),
                pltpu.SemaphoreType.DMA((NT,)),
                pltpu.SemaphoreType.DMA((NT,)),
                pltpu.SemaphoreType.DMA((2 * NT,)),
                pltpu.SemaphoreType.DMA((2 * NT,)),
                pltpu.SemaphoreType.DMA((6,)),
                pltpu.SemaphoreType.DMA((3 * NT,)),
                pltpu.SemaphoreType.DMA((6,)),
                pltpu.SemaphoreType.DMA((6,)),
                pltpu.SemaphoreType.DMA((NT,)),
                pltpu.SemaphoreType.DMA((NT,)),
            ],
            compiler_params=pltpu.CompilerParams(collective_id=0, has_side_effects=True),
        )(start_states, conduct, velocity)

    in_specs = (P("ta", "gx", "gy"), P("gx", "gy"), P(None, "gx", "gy"))
    return jax.shard_map(
        local, mesh=mesh, in_specs=in_specs, out_specs=P("ta", "gx", "gy"), check_vma=False
    )
```

```python
import functools

import jax
import jax.numpy as jnp
from jax import lax
from jax.experimental import pallas as pl
from jax.experimental.pallas import tpu as pltpu
from jax.sharding import PartitionSpec as P

MESH = pl.DeviceIdType.MESH
NT = 8
TR = 64
TC = 512
LT = 128
HB = 24
RAD = 18
ORDER = (4, 5, 3, 7, 2, 6, 1, 0)
WR = TR + 2 * HB
ER = 32
ROWS = [(0, 0, RAD), (1, 4, 16), (5, 7, 8)]
FULL = (0, WR)
SPAN = (8, WR - 16)
LAST = (16, WR - 32)
EDGE = {1: (0, 8), 0: (8, 16), -1: (24, 8)}


def roll(value, shift, axis):
    return pltpu.roll(value, shift % value.shape[axis], axis)


def fold(read, base):
    lane = lax.broadcasted_iota(jnp.int32, (8, LT), 1)
    parts = []
    for start, groups in ((40, 3), (0, 4), (32, 4), (0, 3)):
        value = roll(read(start), base, 1)
        for group in range(1, groups):
            moved = roll(read(start + 8 * group), base + 32 * group, 1)
            value = jnp.where(lane < 32 * group, value, moved)
        parts.append(value)
    return parts


def unfold(read, base):
    for start, groups, first in ((0, 3, 0), (8, 4, 3), (16, 4, 7), (24, 3, 11)):
        value = read(start)
        for group in range(groups):
            yield first + group, roll(value, base - 32 * group, 1)


def kernel(
    gxn, gyn, u_ref, cond_ref, vel_ref, out_ref,
    ubuf, wbuf, xbuf, ebuf, xedge, main, other, cwin, cfull, cfold, cedge, coef, state, half, fsend, frecv,
    load_sem, s_main, r_main, s_strip, r_strip, s_edge, r_edge, sc, rc, sf, rf,
):
    ta = lax.axis_index("ta")
    gx = lax.axis_index("gx")
    gy = lax.axis_index("gy")
    even = lax.rem(ta, 2) == 0
    tile_m = ta // 2
    tile_o = lax.rem(tile_m + jnp.where(even, 3, 1), 4)

    def has(dx, dy):
        x, y = gx + dx, gy + dy
        return (x >= 0) & (x < gxn) & (y >= 0) & (y < gyn)

    def ring(step):
        return lax.rem(ta + step, NT)

    def mirror(step):
        return ring(jnp.where(even, step, NT - step))

    barrier = pltpu.get_barrier_semaphore()

    def greet(section, dx, dy):
        pl.semaphore_signal(
            barrier, inc=1, device_id=(section, gx + dx, gy + dy), device_id_type=MESH
        )

    for dx in (-1, 1):

        @pl.when(has(dx, 0))
        def _():
            for step in range(NT):
                greet(ring(step), dx, 0)

    for owner, dy in ((0, -1), (NT - 1, 1)):
        for dx in (-1, 0, 1):

            @pl.when((ta == owner) & has(dx, dy))
            def _():
                for step in range(NT):
                    greet(ring(step), dx, dy)

    for step in range(1, NT):
        greet(ring(step), 0, 0)

    lanes_m = pl.ds(pl.multiple_of(tile_m * LT, LT), LT)
    lanes_o = pl.ds(pl.multiple_of(tile_o * LT, LT), LT)
    loads = [
        pltpu.make_async_copy(u_ref.at[0], ubuf, load_sem.at[0]),
        pltpu.make_async_copy(cond_ref.at[:, lanes_m], main.at[0], load_sem.at[1]),
        pltpu.make_async_copy(cond_ref.at[:, lanes_o], other.at[0], load_sem.at[2]),
        pltpu.make_async_copy(vel_ref.at[:, :, lanes_m], main.at[pl.ds(1, 2)], load_sem.at[3]),
        pltpu.make_async_copy(vel_ref.at[:, :, lanes_o], other.at[pl.ds(1, 2)], load_sem.at[4]),
    ]
    for load in loads:
        load.start()

    count = NT - 1
    for dx in (-1, 1):
        count = count + NT * has(dx, 0).astype(jnp.int32)
    for dy in (-1, 1):
        for dx in (-1, 0, 1):
            count = count + has(dx, dy).astype(jnp.int32)

    xbuf[0, 0:6, :] = jnp.zeros((6, LT), jnp.float32)
    xbuf[0, WR - 6 : WR, :] = jnp.zeros((6, LT), jnp.float32)
    cwin[:, 0:6, :] = jnp.zeros((3, 6, LT), jnp.float32)
    cwin[:, WR - 6 : WR, :] = jnp.zeros((3, 6, LT), jnp.float32)

    def clear(ref, planes, start, rows):
        ref[:, start : start + rows, :] = jnp.zeros((planes, rows, LT), jnp.float32)

    for dx, start in ((1, 0), (-1, HB + TR)):

        @pl.when(jnp.logical_not(has(-dx, 0)))
        def _():
            clear(xbuf, NT, start, HB)
            clear(cwin, 3, start, HB)

    for owner, dy in ((0, 1), (NT - 1, -1)):
        for dx in (-1, 0, 1):

            @pl.when((ta == owner) & jnp.logical_not(has(-dx, -dy)))
            def _():
                clear(xedge, NT, *EDGE[dx])
                clear(cedge, 3, *EDGE[dx])

    for load in loads:
        load.wait()

    lane = lax.broadcasted_iota(jnp.int32, (TR, LT), 1)
    for owner in range(NT):
        tile = owner // 2
        if owner % 2 == 0:
            mate, keep = (tile + 3) % 4, lane < 96
        else:
            mate, keep = (tile + 1) % 4, lane >= 32
        wbuf[owner] = jnp.where(
            keep, ubuf[:, tile * LT : (tile + 1) * LT], ubuf[:, mate * LT : (mate + 1) * LT]
        )
    for slot, (first, base) in enumerate(((3 * LT, 32), (0, 0))):
        for at, part in enumerate(fold(lambda start: ubuf[start : start + 8, first : first + LT], base)):
            ebuf[slot, 8 * at : 8 * at + 8] = part
    use_m = jnp.where(even, lane, LT - 1 - lane) < 96
    for part in range(3):
        cwin[part, HB : HB + TR, :] = jnp.where(use_m, main[part], other[part])
    for owner, base in ((0, 32), (NT - 1, 0)):

        @pl.when(ta == owner)
        def _():
            for part in range(3):
                for at, value in enumerate(fold(lambda start: other[part, start : start + 8], base)):
                    cfold[part, 8 * at : 8 * at + 8] = value

    xbuf[ta, HB : HB + TR] = wbuf[ta]
    pl.semaphore_wait(barrier, count)

    def main_copy(owner, section):
        return pltpu.make_async_remote_copy(
            src_ref=wbuf.at[owner],
            dst_ref=xbuf.at[section, pl.ds(HB, TR)],
            send_sem=s_main.at[owner],
            recv_sem=r_main.at[section],
            device_id=(owner, gx, gy),
            device_id_type=MESH,
        )

    def strip_copy(owner, section, dx, rows, here=False):
        if dx < 0:
            src, dst = pl.ds(0, rows), pl.ds(HB + TR, rows)
        else:
            src, dst = pl.ds(TR - rows, rows), pl.ds(HB - rows, rows)
        side = (dx + 1) // 2
        return pltpu.make_async_remote_copy(
            src_ref=wbuf.at[owner, src],
            dst_ref=xbuf.at[section, dst],
            send_sem=s_strip.at[NT * side + owner],
            recv_sem=r_strip.at[NT * side + section],
            device_id=(ta, gx, gy) if here else (owner, gx + dx, gy),
            device_id_type=MESH,
        )

    def edge_copy(section, dx, dy, here=False):
        slot, owner = (0, 0) if dy > 0 else (1, NT - 1)
        start, rows = EDGE[dx]
        return pltpu.make_async_remote_copy(
            src_ref=ebuf.at[slot, pl.ds(start, rows)],
            dst_ref=xedge.at[section, pl.ds(start, rows)],
            send_sem=s_edge.at[3 * slot + dx + 1],
            recv_sem=r_edge.at[3 * section + dx + 1],
            device_id=(ta, gx, gy) if here else (ring(lax.rem(owner + NT - ta, NT)), gx + dx, gy + dy),
            device_id_type=MESH,
        )

    def coef_copy(dx, dy, here=False):
        if dy == 0:
            if dx < 0:
                src, dst = pl.ds(HB, RAD), pl.ds(HB + TR, RAD)
            else:
                src, dst = pl.ds(HB + TR - RAD, RAD), pl.ds(HB - RAD, RAD)
            src, dst = cwin.at[:, src, :], cwin.at[:, dst, :]
        else:
            place = pl.ds(*EDGE[dx])
            src, dst = cfold.at[:, place, :], cedge.at[:, place, :]
        at = 3 * (1 if dy else 0) + dx + 1
        return pltpu.make_async_remote_copy(
            src_ref=src,
            dst_ref=dst,
            send_sem=sc.at[at],
            recv_sem=rc.at[at],
            device_id=(ta, gx, gy) if here else (ta, gx + dx, gy + dy),
            device_id_type=MESH,
        )

    coef_dirs = [(-1, 0, None), (1, 0, None)]
    coef_dirs += [(dx, 1, 0) for dx in (-1, 0, 1)] + [(dx, -1, NT - 1) for dx in (-1, 0, 1)]

    def sends(act):
        for dx in (-1, 1, 0):
            for dy in (-1, 1):

                @pl.when(has(dx, dy))
                def _():
                    act(edge_copy(ta, dx, dy))

        for first, last, rows in ROWS:

            @pl.when((ta >= first) & (ta <= last))
            def _():
                for step in ORDER:
                    for dx in (-1, 1):

                        @pl.when(has(dx, 0))
                        def _():
                            act(strip_copy(mirror(step), ta, dx, rows))

        for dx, dy, only in coef_dirs:
            near = has(dx, dy)

            @pl.when(near if only is None else near & (ta == only))
            def _():
                act(coef_copy(dx, dy))

        for step in (4, 5, 3, 7, 2, 6, 1):
            act(main_copy(mirror(step), ta))

    sends(lambda copy: copy.start())

    for dx, dy, only in coef_dirs:
        near = has(-dx, -dy)

        @pl.when(near if only is None else near & (ta == only))
        def _():
            coef_copy(dx, dy, True).wait_recv()

    cfull[...] = cwin[...]
    edge_lane = lax.broadcasted_iota(jnp.int32, (8, LT), 1)
    for owner, base in ((0, 96), (NT - 1, 0)):

        @pl.when(ta == owner)
        def _():
            mine = (edge_lane >= base) & (edge_lane < base + 32)
            for part in range(3):
                for at, value in unfold(lambda start: cedge[part, start : start + 8], base):
                    rows = slice(8 * at, 8 * at + 8)
                    cfull[part, rows] = jnp.where(mine, value, cfull[part, rows])

    wlane = lax.broadcasted_iota(jnp.int32, (WR, LT), 1)
    row = lax.broadcasted_iota(jnp.int32, (WR, LT), 0)

    def mean(part):
        value = cfull[part]
        value = value + roll(value, -1, 1)
        return value + roll(value, -1, 0)

    stiff = mean(0) * (0.25 * 0.1 / 6.0)
    vx = mean(1) * (0.25 * 0.1 / 8.0)
    vy = mean(2) * (0.25 * 0.1 / 8.0)
    gam = vx + vy
    kap = vx - vy
    column = (
        gy * TC + ta * 64 + jnp.where(
            even,
            jnp.where(wlane < 96, wlane, wlane - LT),
            jnp.where(wlane < 32, wlane + 64, wlane - 64),
        )
    )
    line = gx * TR + row - HB
    inside = (column >= 0) & (column < gyn * TC) & (line >= 0) & (line < gxn * TR)

    def put(slot, shift, value):
        coef[slot] = roll(jnp.where(inside, value, 0.0), shift, 0)

    def before(value):
        return roll(value, 1, 0)

    def left(value):
        return roll(value, 1, 1)

    put(0, 0, (4.0 * stiff - gam) + before(4.0 * stiff + kap) + left(4.0 * stiff - kap + before(4.0 * stiff + gam)))
    put(1, 0, (-stiff - kap) + before(gam - stiff))
    put(2, 0, left((-stiff - gam) + before(kap - stiff)))
    put(3, 1, (kap - stiff) + left(gam - stiff))
    put(4, 1, gam - 2.0 * stiff)
    put(5, 1, left(kap - 2.0 * stiff))
    put(6, -1, before((-stiff - gam) + left(-stiff - kap)))
    put(7, -1, before(-kap - 2.0 * stiff))
    put(8, -1, left(before(-gam - 2.0 * stiff)))

    def rate(value, span):
        start, rows = span
        high = roll(value, -1, 1)
        low = roll(value, 1, 1)

        def line_sum(slot):
            return (
                coef[slot, start : start + rows] * value
                + coef[slot + 1, start : start + rows] * high
                + coef[slot + 2, start : start + rows] * low
            )

        return line_sum(0) + roll(line_sum(3), -1, 0) + roll(line_sum(6), 1, 0)

    def trim(value, old, new):
        skip = new[0] - old[0]
        return value[skip : skip + new[1]]

    def result_copy(section):
        return pltpu.make_async_remote_copy(
            src_ref=fsend.at[section],
            dst_ref=frecv.at[ta],
            send_sem=sf.at[section],
            recv_sem=rf.at[ta],
            device_id=(section, gx, gy),
            device_id_type=MESH,
        )

    flane = lax.broadcasted_iota(jnp.int32, (TR // 2, LT), 1)
    fmain = jnp.where(even, flane, LT - 1 - flane) < 64
    def arrive(section, halo, span):
        @pl.when(ta != section)
        def _():
            main_copy(section, section).wait_recv()

        for dx in (-1, 1):

            @pl.when(has(-dx, 0))
            def _():
                strip_copy(section, section, dx, halo, True).wait_recv()

        for owner, dy, base in ((0, 1, 96), (NT - 1, -1, 0)):

            @pl.when(ta == owner)
            def _():
                for dx in (-1, 0, 1):

                    @pl.when(has(-dx, -dy))
                    def _():
                        edge_copy(section, dx, dy, True).wait_recv()

                mine = (edge_lane >= base) & (edge_lane < base + 32)
                for at, value in unfold(lambda start: xedge[section, start : start + 8], base):
                    if span[0] <= 8 * at < span[0] + span[1]:
                        place = slice(8 * at, 8 * at + 8)
                        xbuf[section, place] = jnp.where(mine, value, xbuf[section, place])

        value = xbuf[section, span[0] : span[0] + span[1]]
        return 0.5 * rate(value - 0.25 * rate(value, span), span)

    def advance(value, half, span):
        return value - 2.0 * rate(value - rate(value - half, span), span)

    def give(section, value, span):
        tile = trim(value, span, (HB, TR))
        fsend[section] = jnp.where(fmain, tile[: TR // 2], roll(tile[TR // 2 :], 64, 1))

        @pl.when(ta != section)
        def _():
            result_copy(section).start()

    inner = slice(SPAN[0], SPAN[0] + SPAN[1])
    last = slice(LAST[0], LAST[0] + LAST[1])
    half[...] = arrive(0, RAD, FULL)
    state[inner] = xbuf[0, inner]

    def step(section, carry, halo, span):
        rows = slice(span[0], span[0] + span[1])
        after = arrive(section, halo, span)
        value = advance(state[rows], half[rows], span)
        state[rows] = value
        half[rows] = after
        give(section - 1, value, span)
        return carry

    lax.fori_loop(1, 5, functools.partial(step, halo=16, span=SPAN), 0)
    lax.fori_loop(5, NT, functools.partial(step, halo=8, span=LAST), 0)
    give(NT - 1, advance(state[last], half[last], LAST), LAST)

    frecv[ta] = fsend[ta]

    sends(lambda copy: copy.wait_send())
    for step in range(1, NT):
        result_copy(lax.rem(ta + step, NT)).wait_send()

    for step in range(1, NT):
        peer = lax.rem(ta + step, NT)
        pltpu.make_async_remote_copy(
            src_ref=fsend.at[peer],
            dst_ref=frecv.at[peer],
            send_sem=sf.at[peer],
            recv_sem=rf.at[peer],
            device_id=(peer, gx, gy),
            device_id_type=MESH,
        ).wait_recv()

    for tile in range(4):
        lower, upper = frecv[2 * tile], frecv[2 * tile + 1]
        lanes = slice(tile * LT, (tile + 1) * LT)
        out_ref[0, : TR // 2, lanes] = jnp.where(flane < 64, lower, upper)
        out_ref[0, TR // 2 :, lanes] = roll(jnp.where(flane < 64, upper, lower), 64, 1)


def solution(mesh):
    gxn, gyn = mesh.shape["gx"], mesh.shape["gy"]

    def local(start_states, conduct, velocity):
        return pl.pallas_call(
            functools.partial(kernel, gxn, gyn),
            out_shape=pltpu.VMEM((1, TR, TC), jnp.float32),
            in_specs=[pl.BlockSpec(memory_space=pl.ANY)] * 3,
            out_specs=pl.BlockSpec(memory_space=pltpu.VMEM),
            scratch_shapes=[
                pltpu.VMEM((TR, TC), jnp.float32),
                pltpu.VMEM((NT, TR, LT), jnp.float32),
                pltpu.VMEM((NT, WR, LT), jnp.float32),
                pltpu.VMEM((2, ER, LT), jnp.float32),
                pltpu.VMEM((NT, ER, LT), jnp.float32),
                pltpu.VMEM((3, TR, LT), jnp.float32),
                pltpu.VMEM((3, TR, LT), jnp.float32),
                pltpu.VMEM((3, WR, LT), jnp.float32),
                pltpu.VMEM((3, WR, LT), jnp.float32),
                pltpu.VMEM((3, ER, LT), jnp.float32),
                pltpu.VMEM((3, ER, LT), jnp.float32),
                pltpu.VMEM((9, WR, LT), jnp.float32),
                pltpu.VMEM((WR, LT), jnp.float32),
                pltpu.VMEM((WR, LT), jnp.float32),
                pltpu.VMEM((NT, TR // 2, LT), jnp.float32),
                pltpu.VMEM((NT, TR // 2, LT), jnp.float32),
                pltpu.SemaphoreType.DMA((5,)),
                pltpu.SemaphoreType.DMA((NT,)),
                pltpu.SemaphoreType.DMA((NT,)),
                pltpu.SemaphoreType.DMA((2 * NT,)),
                pltpu.SemaphoreType.DMA((2 * NT,)),
                pltpu.SemaphoreType.DMA((6,)),
                pltpu.SemaphoreType.DMA((3 * NT,)),
                pltpu.SemaphoreType.DMA((6,)),
                pltpu.SemaphoreType.DMA((6,)),
                pltpu.SemaphoreType.DMA((NT,)),
                pltpu.SemaphoreType.DMA((NT,)),
            ],
            compiler_params=pltpu.CompilerParams(collective_id=0, has_side_effects=True),
        )(start_states, conduct, velocity)

    in_specs = (P("ta", "gx", "gy"), P("gx", "gy"), P(None, "gx", "gy"))
    return jax.shard_map(
        local, mesh=mesh, in_specs=in_specs, out_specs=P("ta", "gx", "gy"), check_vma=False
    )
```
